256 devices in a mesh: theta: 128 (over z, x_lo, y, core), inst: 2 (over x_hi).
Axes of the slice: x: 4 (x_hi: 2, x_lo: 2; x = x_hi * 2 + x_lo), y: 4, z: 8, core: 2. Of those that a mesh axis runs over, the one named last changes fastest.
Arguments:
- coarse_state: float32 [5, 9, 65536], P(None, None, ('theta', 'inst')), may hold values from -6 to 6
- send_cells: int32 [256, 2048], P(('theta', 'inst')), may hold values from -1 to 255, as said below
- fine_source: int32 [2, 524288], P(None, ('theta', 'inst')), may hold values from 0 to 2047, as said below
- intersection_weight: float32 [524288], P(('theta', 'inst')), may hold values from 0.2 to 0.8
- neighbours: int32 [6, 524288], P(None, ('theta', 'inst')), may hold values from 0 to 3583, as said below
- face_area: float32 [6, 524288], P(None, ('theta', 'inst')), may hold values from 0.25 to 2
- time_step: float32 [524288], P(('theta', 'inst')), may hold values from 0.02 to 0.1
- face_mixing: float32 [6, 5, 5], replicated, may hold values from -0.75 to 1.2
- frequency: float32 [1], replicated, may hold values from 1 to 3
Outputs:
- fine_state: float32 [5, 9, 524288], P(None, None, ('theta', 'inst'))
The draws below stay inside these ranges and needn't reach their ends.
Inputs may be any that keep to these rules, and one draw needn't show every extreme that they name: `send_cells`: entry [o, d * 8 + s] is the coarse cell of block o (numbered 0 to 255 within the block) that block o sends toward fine block d in slot s, or -1 where the slot is empty; the live slots of each pair come first, every pair has 1 to 8 live slots, and some fine block receives 8 live slots from every coarse block. `fine_source`: an entry o * 8 + s of a cell of fine block d names a live slot of send_cells[o] toward d; every live slot toward d is named by some cell of d. `neighbours`: A cell's own position in the extended list is 512 plus its index in the block. A position p below 3072 lies in layer p // 512 - 1, a position 3072 + q in layer q // 128; a cell of layer l names only positions of layers l - 1, l and l + 1, and positions at or above 3072 only of layer l.
All inputs are finite; a program needn't handle non-finite values.
Results may differ from the reference program's by a relative error of at most 0.0003.
Values sent between devices are 32-bit elements; how exact they have to be, the bound alone decides.
A program may use at most 128 MiB of HBM per device.

```python
import math
import jax
import jax.numpy as jnp
from jax import lax

NV = 5
NI = 9
AXIAL = 128
RAD = 4
LAYERS = 4
CAP = 8
NBLOCK = 256
RIM = 512
CELLS = 2048
CCELLS = 256
NCELLS = 524288
NCOARSE = 65536
N_THETA = 128
N_INST = 2


def live_counts(key):
    counts = jax.random.randint(jax.random.fold_in(key, 11), (NBLOCK, NBLOCK), 1, CAP + 1)
    full_dest = jax.random.randint(jax.random.fold_in(key, 13), (), 0, NBLOCK)
    dest_ids = jnp.arange(NBLOCK, dtype=jnp.int32)
    return jnp.where(dest_ids[None, :] == full_dest, CAP, counts).astype(jnp.int32)


def draw_send_cells(key, part):
    counts = live_counts(key)
    cell_picks = jax.random.randint(jax.random.fold_in(key, 17), (NBLOCK, NBLOCK, CAP), 0, CCELLS)
    slot_ids = jnp.arange(CAP, dtype=jnp.int32)
    live_mask = slot_ids[None, None, :] < counts[:, :, None]
    return jnp.where(live_mask, cell_picks, -1).reshape(NBLOCK, NBLOCK * CAP).astype(jnp.int32)


def sources_for(dest_key, column):
    slot_ids = jnp.arange(CAP, dtype=jnp.int32)
    live_mask = (slot_ids[None, :] < column[:, None]).reshape(-1)
    live_order = jnp.argsort(jnp.where(live_mask, 0, 1), stable=True).astype(jnp.int32)
    live_total = jnp.sum(live_mask.astype(jnp.int32))
    spread = jax.random.permutation(jax.random.fold_in(dest_key, 1), CELLS).astype(jnp.int32)
    first_pick = live_order[spread % live_total]
    second_pick = live_order[jax.random.randint(jax.random.fold_in(dest_key, 2), (CELLS,), 0, live_total)]
    return jnp.stack([first_pick, second_pick])


def draw_fine_source(key, part):
    counts = live_counts(key)
    dest_keys = jax.random.split(jax.random.fold_in(key, 19), NBLOCK)
    per_dest = jax.vmap(sources_for)(dest_keys, counts.T)
    return per_dest.transpose(1, 0, 2).reshape(2, NBLOCK * CELLS).astype(jnp.int32)


def draw_neighbours(key, part):
    cell_index = jnp.arange(NBLOCK * CELLS, dtype=jnp.int32)
    half_side = cell_index // CELLS % 2
    in_block = cell_index % CELLS
    layer_id = in_block // RIM
    row_id = in_block // AXIAL % RAD
    col_id = in_block % AXIAL
    own_pos = RIM + in_block
    jogs = jax.random.randint(jax.random.fold_in(key, 3), (2, NBLOCK * CELLS), -2, 3)
    behind_pos = layer_id * RIM + row_id * AXIAL + jnp.clip(col_id + jogs[0], 0, AXIAL - 1)
    ahead_pos = (layer_id + 2) * RIM + row_id * AXIAL + jnp.clip(col_id + jogs[1], 0, AXIAL - 1)
    across_pos = 2 * RIM + CELLS + layer_id * AXIAL + col_id
    outward = jnp.where(row_id < RAD - 1, own_pos + AXIAL, jnp.where(half_side == 0, across_pos, own_pos))
    inward = jnp.where(row_id > 0, own_pos - AXIAL, jnp.where(half_side == 1, across_pos, own_pos))
    upward = jnp.where(col_id < AXIAL - 1, own_pos + 1, own_pos)
    downward = jnp.where(col_id > 0, own_pos - 1, own_pos)
    stacked = jnp.stack([behind_pos, ahead_pos, outward, inward, upward, downward])
    wall_mask = jax.random.randint(jax.random.fold_in(key, 5), stacked.shape, 0, 16) == 0
    return jnp.where(wall_mask, own_pos[None, :], stacked).astype(jnp.int32)


def draw_face_mixing(key, part):
    identity = jnp.eye(NV, dtype=jnp.float32)[None, :, :]
    diagonal = jax.random.uniform(jax.random.fold_in(key, 23), (6, NV, NV), minval=0.6, maxval=1.2)
    coupling = jnp.clip(0.2 * jax.random.normal(jax.random.fold_in(key, 29), (6, NV, NV)), -0.7, 0.7)
    return (identity * diagonal + (1.0 - identity) * coupling).astype(jnp.float32)


def level_of(key, shape, shards, low, largest):
    def one(axis_at, shards_of):
        draws = jax.random.uniform(jax.random.fold_in(jax.random.fold_in(key, 6), axis_at), (shards_of,), jnp.float32, low / len(shards), largest / len(shards))
        return jnp.repeat(jnp.exp(draws), shape[axis_at] // shards_of).reshape((-1,) + (1,) * (len(shape) - axis_at - 1))

    level = one(*shards[0])
    for cut in shards[1:]:
        level = level * one(*cut)
    return level


def normal_values(own_key, dims, width, most, cuts=(), held_as=jnp.bfloat16):
    result = width * jax.random.normal(own_key, dims, jnp.float32)
    if cuts:
        result = result * level_of(own_key, dims, cuts, -0.22, 0.18)
    return jnp.clip(result, -most, most).astype(held_as)


def setup_inputs(seed: int = 0) -> dict:
    seeds = jax.random.split(jax.random.key(seed), 10)
    return {
        "coarse_state": normal_values(seeds[0], (NV, NI, NCOARSE), 1.0, 6.0, ((2, 256),), jnp.float32),
        "send_cells": draw_send_cells(jax.random.fold_in(seeds[9], 71), 0),
        "fine_source": draw_fine_source(jax.random.fold_in(seeds[9], 71), 0),
        "intersection_weight": jnp.clip(0.2 + 0.6 * jax.random.uniform(seeds[3], (NCELLS,), jnp.float32) ** level_of(seeds[3], (NCELLS,), ((0, 256),), -0.2, 0.2), 0.2, 0.8),
        "neighbours": draw_neighbours(jax.random.fold_in(seeds[9], 71), 0),
        "face_area": jnp.clip(jnp.exp(math.log(2.0) - 2.0794415 * jax.random.uniform(seeds[5], (6, NCELLS), jnp.float32) ** level_of(seeds[5], (6, NCELLS), ((1, 256),), -0.2, 0.2)), 0.25, 2.0),
        "time_step": jnp.clip(jnp.exp(math.log(0.1) - 1.609438 * jax.random.uniform(seeds[6], (NCELLS,), jnp.float32) ** level_of(seeds[6], (NCELLS,), ((0, 256),), -0.2, 0.2)), 0.02, 0.1),
        "face_mixing": draw_face_mixing(jax.random.fold_in(seeds[9], 71), 0),
        "frequency": jnp.clip(jax.random.uniform(seeds[8], (1,), jnp.float32, 1.0, 3.0), 1.0, 3.0),
    }


SEGMENT_COEFS = (0.6, 0.6, 1.0)


def spectral_matrix(instances):
    index_row = jnp.arange(instances, dtype=jnp.int32)
    offsets = index_row[:, None] - index_row[None, :]
    parity = jnp.where(jnp.abs(offsets) % 2 == 0, 1.0, -1.0).astype(jnp.float32)
    angles = jnp.pi * offsets.astype(jnp.float32) / instances
    safe_sine = jnp.where(offsets == 0, 1.0, jnp.sin(angles)).astype(jnp.float32)
    return jnp.where(offsets == 0, 0.0, 0.5 * parity / safe_sine).astype(jnp.float32)


def rate_of(fields, extended, nbr_links, face_areas, mixing, omega_rate, time_deriv):
    cell_count = fields.shape[1]
    nearby = jnp.take(extended, nbr_links, axis=1)
    jumps = (nearby - fields[:, None, :]) * face_areas[None, :, :]
    jumps = jumps.reshape(NV, NI, 6, cell_count)
    fluxes = jnp.einsum("kvw,wnkc->vnc", mixing, jumps, precision=lax.Precision.HIGHEST)
    spectral = jnp.einsum("nm,vmc->vnc", time_deriv, fields.reshape(NV, NI, cell_count), precision=lax.Precision.HIGHEST)
    return (omega_rate * spectral - fluxes).reshape(NV * NI, cell_count)


def extended_global(fields):
    var_width = NV * NI
    blocks = fields.reshape(var_width, N_THETA, N_INST, LAYERS, RAD, AXIAL)
    behind_layer = jnp.roll(blocks[:, :, :, LAYERS - 1], 1, axis=1)
    ahead_layer = jnp.roll(blocks[:, :, :, 0], -1, axis=1)
    hub_side = blocks[:, :, 1, :, 0, :]
    tip_side = blocks[:, :, 0, :, RAD - 1, :]
    others = jnp.stack([hub_side, tip_side], axis=2)
    joined = jnp.concatenate([
        behind_layer.reshape(var_width, N_THETA, N_INST, RIM),
        blocks.reshape(var_width, N_THETA, N_INST, CELLS),
        ahead_layer.reshape(var_width, N_THETA, N_INST, RIM),
        others.reshape(var_width, N_THETA, N_INST, LAYERS * AXIAL)], axis=3)
    return joined.reshape(var_width, NBLOCK, -1).transpose(1, 0, 2)


def reference(coarse_state, send_cells, fine_source, intersection_weight, neighbours, face_area, time_step, face_mixing, frequency):
    var_width = NV * NI
    dest_block = jnp.arange(NCELLS, dtype=jnp.int32) // CELLS
    owners = (fine_source // CAP).astype(jnp.int32)
    within = (fine_source % CAP).astype(jnp.int32)
    local_rows = send_cells[owners, dest_block[None, :] * CAP + within]
    coarse_index = (owners * CCELLS + jnp.maximum(local_rows, 0)).astype(jnp.int32)
    coarse_flat = coarse_state.reshape(var_width, NCOARSE)
    first_src = jnp.take(coarse_flat, coarse_index[0], axis=1)
    second_src = jnp.take(coarse_flat, coarse_index[1], axis=1)
    start_field = intersection_weight[None, :] * first_src + (1.0 - intersection_weight[None, :]) * second_src
    time_deriv = spectral_matrix(NI)
    omega_rate = frequency[0]
    link_blocks = neighbours.reshape(6, NBLOCK, CELLS).transpose(1, 0, 2)
    area_blocks = face_area.reshape(6, NBLOCK, CELLS).transpose(1, 0, 2)

    def block_rate(packed):
        ext_block, field_block, link_block, area_block = packed
        return rate_of(field_block, ext_block, link_block, area_block, face_mixing, omega_rate, time_deriv)

    current = start_field
    for segment_coef in SEGMENT_COEFS:
        ext_all = extended_global(current)
        own_all = current.reshape(var_width, NBLOCK, CELLS).transpose(1, 0, 2)
        block_rates = lax.map(block_rate, (ext_all, own_all, link_blocks, area_blocks))
        rate_full = block_rates.transpose(1, 0, 2).reshape(var_width, NCELLS)
        current = start_field - segment_coef * time_step[None, :] * rate_full
    return current.reshape(NV, NI, NCELLS)
```

```python
import functools

import jax
import jax.numpy as jnp
import numpy as np
from jax import lax
from jax.experimental import pallas as pl
from jax.experimental.pallas import tpu as pltpu
from jax.sharding import PartitionSpec as P

NV = 5
NI = 9
AXIAL = 128
RAD = 4
LAYERS = 4
RIM = 512
CELLS = 2048
EXT = CELLS + 2 * RIM
ROWS = 48
SPLIT = 2 * ROWS
TILE = 256
TILES = CELLS // TILE
NEAR = 7
GROUP = 16
SOURCES = 8

SEGMENT_COEFS = (0.6, 0.6, 1.0)
MESH = pl.DeviceIdType.MESH
F32 = jnp.float32
BF16 = jnp.bfloat16


def spectral_rows():
    offsets = np.arange(NI)[:, None] - np.arange(NI)[None, :]
    sine = np.where(offsets == 0, 1.0, np.sin(np.pi * offsets / NI))
    matrix = np.where(offsets == 0, 0.0, 0.5 * np.where(offsets % 2 == 0, 1.0, -1.0) / sine)
    place = np.array([[v * 8 + n if n < 8 else NV * 8 + v for n in range(NI)] for v in range(NV)])
    full = np.zeros((ROWS, ROWS), np.float32)
    for v in range(NV):
        full[np.ix_(place[v], place[v])] = matrix
    high = full.astype(BF16)
    low = (full - high.astype(np.float32)).astype(BF16)
    return np.concatenate([np.concatenate([high, high], 1), np.concatenate([low, low], 1)], 0)


def halves(x):
    high = x.astype(BF16)
    return high, (x - high.astype(F32)).astype(BF16)


def one_hot(low):
    hit = lax.broadcasted_iota(jnp.int32, (TILE, TILE), 0) == low
    return jnp.where(hit, 1.0, 0.0).astype(BF16)


def pick(table, hot, sets, count):
    found = jnp.dot(table, hot, preferred_element_type=F32)
    sets = jnp.broadcast_to(sets, (8, TILE))
    masks = [sets == s for s in range(1, count)]
    rows = []
    for r in range(0, ROWS, 8):
        parts = []
        for base in (r, ROWS + r):
            value = found[base : base + 8]
            for s in range(1, count):
                value = jnp.where(masks[s - 1], found[s * SPLIT + base : s * SPLIT + base + 8], value)
            parts.append(value)
        rows.append(parts[0] + parts[1])
    return rows


def kernel(
    coarse, send, fsrc, weight, nbr, area, dt, mix, freq, dmat, out,
    outg, recv1, send2, recv2, rtab, ohs, ohn, near, sidn, sids, field, halo, radial, mixcol,
    ssem1, rsem1, ssem2, rsem2, hssem, hrsem,
):
    t = lax.axis_index("theta")
    i = lax.axis_index("inst")
    count = 128
    g = t // 8
    h = (t % 8) * 2 + i

    def in_phase1(s):
        return ((g + s) % GROUP) * 8 + t % 8, i

    def in_phase2(s):
        other = (h + s) % GROUP
        return g * 8 + other // 2, other % 2

    ahead = ((t + 1) % count, i)
    behind = ((t + count - 1) % count, i)
    partner = (t, 1 - i)

    barrier = pltpu.get_barrier_semaphore()
    for s in range(1, GROUP):
        pl.semaphore_signal(barrier, inc=1, device_id=in_phase1(s), device_id_type=MESH)
        pl.semaphore_signal(barrier, inc=1, device_id=in_phase2(s), device_id_type=MESH)
    pl.semaphore_signal(barrier, inc=1, device_id=ahead, device_id_type=MESH)
    pl.semaphore_signal(barrier, inc=1, device_id=behind, device_id_type=MESH)

    rows = jnp.concatenate(
        [coarse[v, 0:8, :] for v in range(NV)]
        + [coarse[v, 8:9, :] for v in range(NV)]
        + [jnp.zeros((ROWS - NV * NI, TILE), F32)],
        axis=0,
    )
    table = jnp.concatenate(halves(rows), axis=0)

    def gather_out(c, carry):
        low = jnp.maximum(send[:, pl.ds(pl.multiple_of(c * TILE, TILE), TILE)], 0)
        found = jnp.dot(table, one_hot(low), preferred_element_type=F32)
        found = found[:ROWS] + found[ROWS:]
        outg[2 * c] = found[:, :128]
        outg[2 * c + 1] = found[:, 128:]
        return carry

    lax.fori_loop(0, TILES, gather_out, 0)

    pl.semaphore_wait(barrier, 2 * (GROUP - 1) + 2)

    def phase1(s):
        return pltpu.make_async_remote_copy(
            src_ref=outg.at[(g + s) % GROUP],
            dst_ref=recv1.at[g],
            send_sem=ssem1.at[s],
            recv_sem=rsem1.at[s],
            device_id=in_phase1(s),
            device_id_type=MESH,
        )

    def phase2(s):
        return pltpu.make_async_remote_copy(
            src_ref=send2.at[(h + s) % GROUP],
            dst_ref=recv2.at[h],
            send_sem=ssem2.at[s],
            recv_sem=rsem2.at[s],
            device_id=in_phase2(s),
            device_id_type=MESH,
        )

    for s in range(1, GROUP):
        phase1(s).start()
    recv1[g] = outg[g]

    slots = fsrc[...]
    places = ((slots >> 3) & 15) * 128 + (slots >> 7) * 8 + (slots & 7)
    sids[...] = places >> 8
    links = nbr[...]
    layer = lax.broadcasted_iota(jnp.int32, (6, CELLS), 1) >> 9
    sidn[...] = jnp.where(links >= EXT, NEAR - 1, (links >> 8) - 2 * layer)

    def hot_start(c, carry):
        cells = pl.ds(pl.multiple_of(c * TILE, TILE), TILE)
        for side in range(2):
            q = fsrc[side : side + 1, cells]
            ohs[side, c] = one_hot((((q >> 3) & 1) * 128) + (q >> 7) * 8 + (q & 7))
        for k in range(6):
            ohn[k, c] = one_hot(nbr[k : k + 1, cells] & 255)
        return carry

    lax.fori_loop(0, TILES, hot_start, 0)
    sub = lax.broadcasted_iota(jnp.int32, (8, 128), 0)
    for k in range(6):
        for w in range(NV):
            column = jnp.zeros((8, 128), F32)
            for v in range(NV):
                column = jnp.where(sub == v, mix[k, v, w], column)
            mixcol[k, w] = column

    for s in range(1, GROUP):
        phase1(s).wait_recv()

    lane = lax.broadcasted_iota(jnp.int32, (8, 128), 1)

    def turn(r, carry):
        part = pl.ds(pl.multiple_of(r * 8, 8), 8)
        x = [recv1[j, part, :] for j in range(GROUP)]
        for bit in range(4):
            step = 8 << bit
            keep = (lane & step) == 0
            for a in range(GROUP):
                b = a | (1 << bit)
                if a != b:
                    low = jnp.where(keep, x[a], pltpu.roll(x[b], step, 1))
                    high = jnp.where(keep, pltpu.roll(x[a], 128 - step, 1), x[b])
                    x[a], x[b] = low, high
        for j in range(GROUP):
            send2[j, part, :] = x[j]
        return carry

    lax.fori_loop(0, ROWS // 8, turn, 0)

    for s in range(1, GROUP):
        phase2(s).start()
    recv2[h] = send2[h]
    for s in range(1, GROUP):
        phase2(s).wait_recv()

    for s in range(SOURCES):
        for side in range(2):
            high, low = halves(recv2[2 * s + side])
            rtab[s * SPLIT : s * SPLIT + ROWS, side * 128 : side * 128 + 128] = high
            rtab[s * SPLIT + ROWS : (s + 1) * SPLIT, side * 128 : side * 128 + 128] = low

    def start_tile(c, carry):
        cells = pl.ds(pl.multiple_of(c * TILE, TILE), TILE)
        first = pick(rtab[...], ohs[0, c], sids[0:1, cells], SOURCES)
        second = pick(rtab[...], ohs[1, c], sids[1:2, cells], SOURCES)
        share = jnp.broadcast_to(weight[:, cells], (8, TILE))
        for r in range(ROWS // 8):
            field[0, 8 * r : 8 * r + 8, cells] = share * first[r] + (1.0 - share) * second[r]
        return carry

    lax.fori_loop(0, TILES, start_tile, 0)

    my_row = jnp.where(i == 0, RAD - 1, 0) * AXIAL

    def exchanges(seg):
        copies = [
            pltpu.make_async_remote_copy(
                src_ref=field.at[seg, :, pl.ds((LAYERS - 1) * RIM, RIM)],
                dst_ref=halo.at[seg, 0],
                send_sem=hssem.at[seg, 0],
                recv_sem=hrsem.at[seg, 0],
                device_id=ahead,
                device_id_type=MESH,
            ),
            pltpu.make_async_remote_copy(
                src_ref=field.at[seg, :, pl.ds(0, RIM)],
                dst_ref=halo.at[seg, 1],
                send_sem=hssem.at[seg, 1],
                recv_sem=hrsem.at[seg, 1],
                device_id=behind,
                device_id_type=MESH,
            ),
        ]
        for a in range(LAYERS):
            copies.append(
                pltpu.make_async_remote_copy(
                    src_ref=field.at[seg, :, pl.ds(pl.multiple_of(a * RIM + my_row, AXIAL), AXIAL)],
                    dst_ref=radial.at[seg, :, pl.ds(a * AXIAL, AXIAL)],
                    send_sem=hssem.at[seg, 2 + a],
                    recv_sem=hrsem.at[seg, 2 + a],
                    device_id=partner,
                    device_id_type=MESH,
                )
            )
        return copies

    def put(layer_at, half, values):
        high, low = halves(values)
        for a in range(max(layer_at - 1, 0), min(layer_at + 2, LAYERS)):
            base = (2 * (layer_at - a + 1) + half) * SPLIT
            near[a, base : base + ROWS, :] = high
            near[a, base + ROWS : base + SPLIT, :] = low

    omega = freq[0]
    for seg in range(3):
        copies = exchanges(seg)
        for copy in copies:
            copy.start()
        for a in range(LAYERS):
            for half in range(2):
                put(a, half, field[seg, :, a * RIM + half * TILE : a * RIM + (half + 1) * TILE])
        for copy in copies:
            copy.wait_recv()
        for half in range(2):
            put(-1, half, halo[seg, 0, :, half * TILE : (half + 1) * TILE])
            put(LAYERS, half, halo[seg, 1, :, half * TILE : (half + 1) * TILE])
            high, low = halves(radial[seg, :, half * TILE : (half + 1) * TILE])
            base = (NEAR - 1) * SPLIT
            for a in (2 * half, 2 * half + 1):
                near[a, base : base + ROWS, :] = high
                near[a, base + ROWS : base + SPLIT, :] = low

        def rate_tile(c, carry):
            cells = pl.ds(pl.multiple_of(c * TILE, TILE), TILE)
            a = c // 2
            own = [field[seg, 8 * r : 8 * r + 8, cells] for r in range(ROWS // 8)]
            mine = near[a, pl.ds(pl.multiple_of((2 + c % 2) * SPLIT, SPLIT), SPLIT), :]
            turned = jnp.dot(dmat[...], mine, preferred_element_type=F32)
            rate = [omega * (turned[8 * r : 8 * r + 8] + turned[ROWS + 8 * r : ROWS + 8 * r + 8]) for r in range(ROWS // 8)]
            for k in range(6):
                found = pick(near[a], ohn[k, c], sidn[k : k + 1, cells], NEAR)
                face = jnp.broadcast_to(area[k : k + 1, cells], (8, TILE))
                jump = [(found[r] - own[r]) * face for r in range(ROWS // 8)]
                for v in range(NV):
                    flux = mix[k, v, 0] * jump[0]
                    for w in range(1, NV):
                        flux = flux + mix[k, v, w] * jump[w]
                    rate[v] = rate[v] - flux
                last = jnp.zeros((8, TILE), F32)
                for w in range(NV):
                    column = mixcol[k, w]
                    last = last + jnp.concatenate([column, column], axis=1) * jnp.broadcast_to(jump[NV][w : w + 1], (8, TILE))
                rate[NV] = rate[NV] - last
            step = jnp.broadcast_to(SEGMENT_COEFS[seg] * dt[:, cells], (8, TILE))
            for r in range(ROWS // 8):
                after = field[0, 8 * r : 8 * r + 8, cells] - step * rate[r]
                if seg < 2:
                    field[seg + 1, 8 * r : 8 * r + 8, cells] = after
                elif r < NV:
                    out[r, 0:8, cells] = after
                else:
                    for v in range(NV):
                        out[v, 8:9, cells] = after[v : v + 1]
            return carry

        lax.fori_loop(0, TILES, rate_tile, 0)

    for s in range(1, GROUP):
        phase1(s).wait_send()
        phase2(s).wait_send()
    for seg in range(3):
        for copy in exchanges(seg):
            copy.wait_send()


def per_device(coarse_state, send_cells, fine_source, weight, neighbours, face_area, time_step, mixing, frequency):
    vmem = pl.BlockSpec(memory_space=pltpu.VMEM)
    smem = pl.BlockSpec(memory_space=pltpu.SMEM)
    return pl.pallas_call(
        kernel,
        out_shape=jax.ShapeDtypeStruct((NV, NI, CELLS), F32),
        in_specs=[vmem] * 7 + [smem, smem, vmem],
        out_specs=vmem,
        scratch_shapes=[
            pltpu.VMEM((GROUP, ROWS, 128), F32),
            pltpu.VMEM((GROUP, ROWS, 128), F32),
            pltpu.VMEM((GROUP, ROWS, 128), F32),
            pltpu.VMEM((GROUP, ROWS, 128), F32),
            pltpu.VMEM((SOURCES * SPLIT, TILE), BF16),
            pltpu.VMEM((2, TILES, TILE, TILE), BF16),
            pltpu.VMEM((6, TILES, TILE, TILE), BF16),
            pltpu.VMEM((LAYERS, NEAR * SPLIT, TILE), BF16),
            pltpu.VMEM((6, CELLS), jnp.int32),
            pltpu.VMEM((2, CELLS), jnp.int32),
            pltpu.VMEM((3, ROWS, CELLS), F32),
            pltpu.VMEM((3, 2, ROWS, RIM), F32),
            pltpu.VMEM((3, ROWS, RIM), F32),
            pltpu.VMEM((6, NV, 8, 128), F32),
            pltpu.SemaphoreType.DMA((GROUP,)),
            pltpu.SemaphoreType.DMA((GROUP,)),
            pltpu.SemaphoreType.DMA((GROUP,)),
            pltpu.SemaphoreType.DMA((GROUP,)),
            pltpu.SemaphoreType.DMA((3, 6)),
            pltpu.SemaphoreType.DMA((3, 6)),
        ],
        compiler_params=pltpu.CompilerParams(
            collective_id=0, has_side_effects=True, vmem_limit_bytes=40 * 2**20
        ),
        name="grid_sequence",
    )(
        coarse_state,
        send_cells,
        fine_source,
        weight.reshape(1, CELLS),
        neighbours,
        face_area,
        time_step.reshape(1, CELLS),
        mixing,
        frequency,
        jnp.asarray(spectral_rows()),
    )


def solution(mesh):
    placed = (
        P(None, None, ("theta", "inst")),
        P(("theta", "inst"), None),
        P(None, ("theta", "inst")),
        P(("theta", "inst")),
        P(None, ("theta", "inst")),
        P(None, ("theta", "inst")),
        P(("theta", "inst")),
        P(),
        P(),
    )
    return jax.shard_map(
        per_device,
        mesh=mesh,
        in_specs=placed,
        out_specs=P(None, None, ("theta", "inst")),
        check_vma=False,
    )
```

```python
import functools

import jax
import jax.numpy as jnp
import numpy as np
from jax import lax
from jax.experimental import pallas as pl
from jax.experimental.pallas import tpu as pltpu
from jax.sharding import PartitionSpec as P

NV = 5
NI = 9
AXIAL = 128
RAD = 4
LAYERS = 4
RIM = 512
CELLS = 2048
EXT = CELLS + 2 * RIM
ROWS = 48
SPLIT = 2 * ROWS
TILE = 256
TILES = CELLS // TILE
NEAR = 7
GROUP = 16
SOURCES = 8

SEGMENT_COEFS = (0.6, 0.6, 1.0)
MESH = pl.DeviceIdType.MESH
F32 = jnp.float32
BF16 = jnp.bfloat16


def spectral_rows():
    offsets = np.arange(NI)[:, None] - np.arange(NI)[None, :]
    sine = np.where(offsets == 0, 1.0, np.sin(np.pi * offsets / NI))
    matrix = np.where(offsets == 0, 0.0, 0.5 * np.where(offsets % 2 == 0, 1.0, -1.0) / sine)
    place = np.array([[v * 8 + n if n < 8 else NV * 8 + v for n in range(NI)] for v in range(NV)])
    full = np.zeros((ROWS, ROWS), np.float32)
    for v in range(NV):
        full[np.ix_(place[v], place[v])] = matrix
    high = full.astype(BF16)
    low = (full - high.astype(np.float32)).astype(BF16)
    return np.concatenate([np.concatenate([high, high], 1), np.concatenate([low, low], 1)], 0)


def halves(x):
    high = x.astype(BF16)
    return high, (x - high.astype(F32)).astype(BF16)


def one_hot(low):
    hit = lax.broadcasted_iota(jnp.int32, (TILE, TILE), 0) == low
    return jnp.where(hit, 1.0, 0.0).astype(BF16)


def pick(table, hot, sets, count):
    found = jnp.dot(table, hot, preferred_element_type=F32)
    sets = jnp.broadcast_to(sets, (8, TILE))
    masks = [sets == s for s in range(1, count)]
    rows = []
    for r in range(0, ROWS, 8):
        parts = []
        for base in (r, ROWS + r):
            value = found[base : base + 8]
            for s in range(1, count):
                value = jnp.where(masks[s - 1], found[s * SPLIT + base : s * SPLIT + base + 8], value)
            parts.append(value)
        rows.append(parts[0] + parts[1])
    return rows


def kernel(
    coarse, send, fsrc, weight, nbr, area, dt, mix, freq, dmat, out,
    outg, recv1, send2, recv2, rtab, ohs, ohn, near, sidn, sids, field, mixcol,
    ssem1, rsem1, ssem2, rsem2, hssem, hrsem,
):
    t = lax.axis_index("theta")
    i = lax.axis_index("inst")
    count = 128
    g = t // 8
    h = (t % 8) * 2 + i

    def in_phase1(s):
        return ((g + s) % GROUP) * 8 + t % 8, i

    def in_phase2(s):
        other = (h + s) % GROUP
        return g * 8 + other // 2, other % 2

    ahead = ((t + 1) % count, i)
    behind = ((t + count - 1) % count, i)
    partner = (t, 1 - i)

    barrier = pltpu.get_barrier_semaphore()
    for s in range(1, GROUP):
        pl.semaphore_signal(barrier, inc=1, device_id=in_phase1(s), device_id_type=MESH)
        pl.semaphore_signal(barrier, inc=1, device_id=in_phase2(s), device_id_type=MESH)
    pl.semaphore_signal(barrier, inc=1, device_id=ahead, device_id_type=MESH)
    pl.semaphore_signal(barrier, inc=1, device_id=behind, device_id_type=MESH)

    rows = jnp.concatenate(
        [coarse[0:8, v, :] for v in range(NV)] + [coarse[8], jnp.zeros((ROWS - NV * NI, TILE), F32)], axis=0
    )
    table = jnp.concatenate(halves(rows), axis=0)

    def gather_out(c, carry):
        low = jnp.maximum(send[:, pl.ds(pl.multiple_of(c * TILE, TILE), TILE)], 0)
        found = jnp.dot(table, one_hot(low), preferred_element_type=F32)
        found = found[:ROWS] + found[ROWS:]
        outg[2 * c] = found[:, :128]
        outg[2 * c + 1] = found[:, 128:]
        return carry

    lax.fori_loop(0, TILES, gather_out, 0)

    pl.semaphore_wait(barrier, 2 * (GROUP - 1) + 2)

    def phase1(s):
        return pltpu.make_async_remote_copy(
            src_ref=outg.at[(g + s) % GROUP],
            dst_ref=recv1.at[g],
            send_sem=ssem1.at[s],
            recv_sem=rsem1.at[s],
            device_id=in_phase1(s),
            device_id_type=MESH,
        )

    def phase2(s):
        return pltpu.make_async_remote_copy(
            src_ref=send2.at[(h + s) % GROUP],
            dst_ref=recv2.at[h],
            send_sem=ssem2.at[s],
            recv_sem=rsem2.at[s],
            device_id=in_phase2(s),
            device_id_type=MESH,
        )

    for s in range(1, GROUP):
        phase1(s).start()
    recv1[g] = outg[g]

    slots = fsrc[...]
    places = ((slots >> 3) & 15) * 128 + (slots >> 7) * 8 + (slots & 7)
    sids[...] = places >> 8
    links = nbr[...]
    layer = lax.broadcasted_iota(jnp.int32, (6, CELLS), 1) >> 9
    sidn[...] = jnp.where(links >= EXT, NEAR - 1, (links >> 8) - 2 * layer)

    def hot_start(c, carry):
        cells = pl.ds(pl.multiple_of(c * TILE, TILE), TILE)
        for side in range(2):
            q = fsrc[side : side + 1, cells]
            ohs[side, c] = one_hot((((q >> 3) & 1) * 128) + (q >> 7) * 8 + (q & 7))
        for k in range(6):
            ohn[k, c] = one_hot(nbr[k : k + 1, cells] & 255)
        return carry

    lax.fori_loop(0, TILES, hot_start, 0)
    near[:, 12 * SPLIT :, :] = jnp.zeros((2, 2 * SPLIT, TILE), BF16)
    sub = lax.broadcasted_iota(jnp.int32, (8, 128), 0)
    for k in range(6):
        for w in range(NV):
            column = jnp.zeros((8, 128), F32)
            for v in range(NV):
                column = jnp.where(sub == v, mix[v, k, w], column)
            mixcol[k, w] = column

    for s in range(1, GROUP):
        phase1(s).wait_recv()

    lane = lax.broadcasted_iota(jnp.int32, (8, 128), 1)

    def turn(r, carry):
        part = pl.ds(pl.multiple_of(r * 8, 8), 8)
        x = [recv1[j, part, :] for j in range(GROUP)]
        for bit in range(4):
            step = 8 << bit
            keep = (lane & step) == 0
            for a in range(GROUP):
                b = a | (1 << bit)
                if a != b:
                    low = jnp.where(keep, x[a], pltpu.roll(x[b], step, 1))
                    high = jnp.where(keep, pltpu.roll(x[a], 128 - step, 1), x[b])
                    x[a], x[b] = low, high
        for j in range(GROUP):
            send2[j, part, :] = x[j]
        return carry

    lax.fori_loop(0, ROWS // 8, turn, 0)

    for s in range(1, GROUP):
        phase2(s).start()
    recv2[h] = send2[h]
    for s in range(1, GROUP):
        phase2(s).wait_recv()

    for s in range(SOURCES):
        for side in range(2):
            high, low = halves(recv2[2 * s + side])
            rtab[s * SPLIT : s * SPLIT + ROWS, side * 128 : side * 128 + 128] = high
            rtab[s * SPLIT + ROWS : (s + 1) * SPLIT, side * 128 : side * 128 + 128] = low

    my_row = jnp.where(i == 0, RAD - 1, 0) * AXIAL

    def lanes(start, size):
        return pl.ds(pl.multiple_of(start, 128), size)

    def radial_copy(seg, a):
        return pltpu.make_async_remote_copy(
            src_ref=field.at[seg, :, lanes(RIM + a * RIM + my_row, AXIAL)],
            dst_ref=field.at[seg, :, lanes(EXT + a * AXIAL, AXIAL)],
            send_sem=hssem.at[seg, a],
            recv_sem=hrsem.at[seg, a],
            device_id=partner,
            device_id_type=MESH,
        )

    def behind_copy(seg):
        return pltpu.make_async_remote_copy(
            src_ref=field.at[seg, :, pl.ds(RIM, RIM)],
            dst_ref=field.at[seg, :, pl.ds(RIM + CELLS, RIM)],
            send_sem=hssem.at[seg, 4],
            recv_sem=hrsem.at[seg, 4],
            device_id=behind,
            device_id_type=MESH,
        )

    def ahead_copy(seg):
        return pltpu.make_async_remote_copy(
            src_ref=field.at[seg, :, pl.ds(CELLS, RIM)],
            dst_ref=field.at[seg, :, pl.ds(0, RIM)],
            send_sem=hssem.at[seg, 5],
            recv_sem=hrsem.at[seg, 5],
            device_id=ahead,
            device_id_type=MESH,
        )

    def send_layer(seg, j, a):
        radial_copy(seg, a).start()

        @pl.when(j == 0)
        def _():
            behind_copy(seg).start()

        @pl.when(j == 1)
        def _():
            ahead_copy(seg).start()

    def put(side, at, values):
        high, low = halves(jnp.concatenate(values, axis=0))
        near[side, pl.ds(pl.multiple_of(at * SPLIT, 16), ROWS), :] = high
        near[side, pl.ds(pl.multiple_of(at * SPLIT + ROWS, 16), ROWS), :] = low

    def layer_of(j):
        return jnp.where(j == 0, 0, jnp.where(j == 1, LAYERS - 1, j - 1))

    def start_layer(j, carry):
        a = layer_of(j)
        for half in range(2):
            c = 2 * a + half
            cells = lanes(c * TILE, TILE)
            first = pick(rtab[...], ohs[0, c], sids[0:1, cells], SOURCES)
            second = pick(rtab[...], ohs[1, c], sids[1:2, cells], SOURCES)
            share = jnp.broadcast_to(weight[:, cells], (8, TILE))
            begin = [share * x + (1.0 - share) * y for x, y in zip(first, second)]
            for r in range(ROWS // 8):
                field[0, 8 * r : 8 * r + 8, lanes(RIM + c * TILE, TILE)] = begin[r]
            put(0, 2 + c, begin)
        send_layer(0, j, a)
        return carry

    lax.fori_loop(0, LAYERS, start_layer, 0)

    omega = freq[0]

    def rate_layer(at, carry):
        seg = at // LAYERS
        side = seg % 2
        j = at % LAYERS
        a = layer_of(j)

        def arrived(start, at_set):
            for half in range(2):
                put(side, at_set + half, [field[seg, :, start + half * TILE : start + (half + 1) * TILE]])

        @pl.when(j == 0)
        def _():
            ahead_copy(seg).wait_recv()
            arrived(0, 0)

        @pl.when(j == 1)
        def _():
            behind_copy(seg).wait_recv()
            arrived(RIM + CELLS, 10)

        radial_copy(seg, a).wait_recv()
        high, low = halves(field[seg, :, lanes(EXT + a * AXIAL, AXIAL)])
        across = (12 + a // 2) * SPLIT
        column = lanes(a % 2 * AXIAL, AXIAL)
        near[side, pl.ds(pl.multiple_of(across, 16), ROWS), column] = high
        near[side, pl.ds(pl.multiple_of(across + ROWS, 16), ROWS), column] = low

        coef = jnp.where(seg == 2, SEGMENT_COEFS[2], SEGMENT_COEFS[0])
        for half in range(2):
            c = 2 * a + half
            cells = lanes(c * TILE, TILE)
            here = lanes(RIM + c * TILE, TILE)
            own = [field[seg, 8 * r : 8 * r + 8, here] for r in range(ROWS // 8)]
            mine = near[side, pl.ds(pl.multiple_of((2 + c) * SPLIT, 16), SPLIT), :]
            turned = jnp.dot(dmat[...], mine, preferred_element_type=F32)
            rate = [omega * (turned[8 * r : 8 * r + 8] + turned[ROWS + 8 * r : ROWS + 8 * r + 8]) for r in range(ROWS // 8)]
            table = jnp.concatenate(
                [
                    near[side, pl.ds(pl.multiple_of(2 * a * SPLIT, 16), 6 * SPLIT), :],
                    near[side, pl.ds(pl.multiple_of(across, 16), SPLIT), :],
                ],
                axis=0,
            )
            for k in range(6):
                found = pick(table, ohn[k, c], sidn[k : k + 1, cells], NEAR)
                face = jnp.broadcast_to(area[k : k + 1, cells], (8, TILE))
                jump = [(found[r] - own[r]) * face for r in range(ROWS // 8)]
                for v in range(NV):
                    flux = mix[v, k, 0] * jump[0]
                    for w in range(1, NV):
                        flux = flux + mix[v, k, w] * jump[w]
                    rate[v] = rate[v] - flux
                last = jnp.zeros((8, TILE), F32)
                for w in range(NV):
                    column = mixcol[k, w]
                    last = last + jnp.concatenate([column, column], axis=1) * jnp.broadcast_to(jump[NV][w : w + 1], (8, TILE))
                rate[NV] = rate[NV] - last
            step = jnp.broadcast_to(coef * dt[:, cells], (8, TILE))
            after = [field[0, 8 * r : 8 * r + 8, here] - step * rate[r] for r in range(ROWS // 8)]
            for r in range(ROWS // 8):
                field[seg + 1, 8 * r : 8 * r + 8, here] = after[r]
            put(1 - side, 2 + c, after)

        @pl.when(seg < 2)
        def _():
            send_layer(seg + 1, j, a)

        return carry

    lax.fori_loop(0, 3 * LAYERS, rate_layer, 0)

    for v in range(NV):
        out[0:8, v, :] = field[3, 8 * v : 8 * v + 8, RIM : RIM + CELLS]
    out[8] = field[3, 8 * NV : 9 * NV, RIM : RIM + CELLS]

    for s in range(1, GROUP):
        phase1(s).wait_send()
        phase2(s).wait_send()
    for seg in range(3):
        for a in range(LAYERS):
            radial_copy(seg, a).wait_send()
        behind_copy(seg).wait_send()
        ahead_copy(seg).wait_send()


def per_device(coarse_state, send_cells, fine_source, weight, neighbours, face_area, time_step, mixing, frequency):
    vmem = pl.BlockSpec(memory_space=pltpu.VMEM)
    smem = pl.BlockSpec(memory_space=pltpu.SMEM)
    fine = pl.pallas_call(
        kernel,
        out_shape=jax.ShapeDtypeStruct((NI, NV, CELLS), F32),
        in_specs=[vmem] * 7 + [smem, smem, vmem],
        out_specs=vmem,
        scratch_shapes=[
            pltpu.VMEM((GROUP, ROWS, 128), F32),
            pltpu.VMEM((GROUP, ROWS, 128), F32),
            pltpu.VMEM((GROUP, ROWS, 128), F32),
            pltpu.VMEM((GROUP, ROWS, 128), F32),
            pltpu.VMEM((SOURCES * SPLIT, TILE), BF16),
            pltpu.VMEM((2, TILES, TILE, TILE), BF16),
            pltpu.VMEM((6, TILES, TILE, TILE), BF16),
            pltpu.VMEM((2, 14 * SPLIT, TILE), BF16),
            pltpu.VMEM((6, CELLS), jnp.int32),
            pltpu.VMEM((2, CELLS), jnp.int32),
            pltpu.VMEM((4, ROWS, CELLS + 3 * RIM), F32),
            pltpu.VMEM((6, NV, 8, 128), F32),
            pltpu.SemaphoreType.DMA((GROUP,)),
            pltpu.SemaphoreType.DMA((GROUP,)),
            pltpu.SemaphoreType.DMA((GROUP,)),
            pltpu.SemaphoreType.DMA((GROUP,)),
            pltpu.SemaphoreType.DMA((3, 6)),
            pltpu.SemaphoreType.DMA((3, 6)),
        ],
        compiler_params=pltpu.CompilerParams(
            collective_id=0, has_side_effects=True, vmem_limit_bytes=40 * 2**20
        ),
        name="grid_sequence",
    )(
        coarse_state.transpose(1, 0, 2),
        send_cells,
        fine_source,
        weight.reshape(1, CELLS),
        neighbours,
        face_area,
        time_step.reshape(1, CELLS),
        mixing.transpose(1, 0, 2),
        frequency,
        jnp.asarray(spectral_rows()),
    )
    return fine.transpose(1, 0, 2)


def solution(mesh):
    placed = (
        P(None, None, ("theta", "inst")),
        P(("theta", "inst"), None),
        P(None, ("theta", "inst")),
        P(("theta", "inst")),
        P(None, ("theta", "inst")),
        P(None, ("theta", "inst")),
        P(("theta", "inst")),
        P(),
        P(),
    )
    return jax.shard_map(
        per_device,
        mesh=mesh,
        in_specs=placed,
        out_specs=P(None, None, ("theta", "inst")),
        check_vma=False,
    )
```

```python
import functools

import jax
import jax.numpy as jnp
import numpy as np
from jax import lax
from jax.experimental import pallas as pl
from jax.experimental.pallas import tpu as pltpu
from jax.sharding import PartitionSpec as P

NV = 5
NI = 9
AXIAL = 128
RAD = 4
LAYERS = 4
RIM = 512
CELLS = 2048
EXT = CELLS + 2 * RIM
ROWS = 48
SPLIT = 2 * ROWS
TILE = 256
TILES = CELLS // TILE
NEAR = 7
GROUP = 16
CHUNK = 16
CHUNKS = ROWS // CHUNK
SOURCES = 8

SEGMENT_COEFS = (0.6, 0.6, 1.0)
MESH = pl.DeviceIdType.MESH
F32 = jnp.float32
BF16 = jnp.bfloat16


def spectral_rows():
    offsets = np.arange(NI)[:, None] - np.arange(NI)[None, :]
    sine = np.where(offsets == 0, 1.0, np.sin(np.pi * offsets / NI))
    matrix = np.where(offsets == 0, 0.0, 0.5 * np.where(offsets % 2 == 0, 1.0, -1.0) / sine)
    place = np.array([[v * 8 + n if n < 8 else NV * 8 + v for n in range(NI)] for v in range(NV)])
    full = np.zeros((ROWS, ROWS), np.float32)
    for v in range(NV):
        full[np.ix_(place[v], place[v])] = matrix
    high = full.astype(BF16)
    low = (full - high.astype(np.float32)).astype(BF16)
    return np.concatenate([np.concatenate([high, high], 1), np.concatenate([low, low], 1)], 0)


def halves(x):
    high = x.astype(BF16)
    return high, (x - high.astype(F32)).astype(BF16)


def one_hot(low):
    hit = lax.broadcasted_iota(jnp.int32, (TILE, TILE), 0) == low
    return jnp.where(hit, 1.0, 0.0).astype(BF16)


def pick(table, hot, sets, count):
    found = jnp.dot(table, hot, preferred_element_type=F32)
    sets = jnp.broadcast_to(sets, (8, TILE))
    masks = [sets == s for s in range(1, count)]
    rows = []
    for r in range(0, ROWS, 8):
        parts = []
        for base in (r, ROWS + r):
            value = found[base : base + 8]
            for s in range(1, count):
                value = jnp.where(masks[s - 1], found[s * SPLIT + base : s * SPLIT + base + 8], value)
            parts.append(value)
        rows.append(parts[0] + parts[1])
    return rows


def kernel(
    coarse_in, send_in, fsrc_in, weight_in, nbr_in, area_in, dt_in, mix_in, freq_in, dmat_in, out,
    coarse, send, fsrc, weight, nbr, area, dt, mix, freq, dmat, isem, outg, recv1, send2, recv2, rtab, ohs, ohn, near, sidn, sids, field, mixcol,
    ssem1, rsem1, ssem2, rsem2, hssem, hrsem,
):
    inputs = [
        pltpu.make_async_copy(src, dst, isem.at[at])
        for at, (src, dst) in enumerate(
            [
                (coarse_in, coarse), (send_in, send), (fsrc_in, fsrc), (nbr_in, nbr), (mix_in, mix),
                (freq_in, freq), (weight_in, weight), (area_in, area), (dt_in, dt), (dmat_in, dmat),
            ]
        )
    ]
    for copy in inputs:
        copy.start()

    t = lax.axis_index("theta")
    i = lax.axis_index("inst")
    count = 128
    z, x_lo, y, core = t // 16, t // 8 % 2, t // 2 % 4, t % 2
    g = z * 2 + core
    h = y * 4 + x_lo * 2 + i

    def in_phase1(s):
        other = (g + s) % GROUP
        return ((other // 2 * 2 + x_lo) * 4 + y) * 2 + other % 2, i

    def in_phase2(s):
        other = (h + s) % GROUP
        return ((z * 2 + other // 2 % 2) * 4 + other // 4) * 2 + core, other % 2

    ahead = ((t + 1) % count, i)
    behind = ((t + count - 1) % count, i)
    partner = (t, 1 - i)

    def lanes(start, size):
        return pl.ds(pl.multiple_of(start, 128), size)

    barrier = pltpu.get_barrier_semaphore()

    def greet(s, carry):
        pl.semaphore_signal(barrier, inc=1, device_id=in_phase1(s), device_id_type=MESH)
        pl.semaphore_signal(barrier, inc=1, device_id=in_phase2(s), device_id_type=MESH)
        return carry

    lax.fori_loop(1, GROUP, greet, 0)
    pl.semaphore_signal(barrier, inc=1, device_id=ahead, device_id_type=MESH)
    pl.semaphore_signal(barrier, inc=1, device_id=behind, device_id_type=MESH)

    inputs[0].wait()
    inputs[1].wait()

    rows = jnp.concatenate(
        [coarse[0:8, v, :] for v in range(NV)] + [coarse[8], jnp.zeros((ROWS - NV * NI, TILE), F32)], axis=0
    )
    table = jnp.concatenate(halves(rows), axis=0)

    lane = lax.broadcasted_iota(jnp.int32, (8, 128), 1)

    def gather_out(c, carry):
        even = send[:, lanes(c * TILE, 128)]
        odd = send[:, lanes(c * TILE + 128, 128)]
        keep = (lane[:1] & 16) == 0
        first = jnp.where(keep, even, pltpu.roll(odd, 16, 1))
        second = jnp.where(keep, pltpu.roll(even, 112, 1), odd)
        low = jnp.maximum(jnp.concatenate([first, second], axis=1), 0)
        found = jnp.dot(table, one_hot(low), preferred_element_type=F32)
        found = found[:ROWS] + found[ROWS:]
        outg[2 * c] = found[:, :128]
        outg[2 * c + 1] = found[:, 128:]
        return carry

    lax.fori_loop(0, TILES, gather_out, 0)

    pl.semaphore_wait(barrier, 2 * (GROUP - 1) + 2)

    def phase1(c, s):
        part = pl.ds(c * CHUNK, CHUNK)
        return pltpu.make_async_remote_copy(
            src_ref=outg.at[(g + s) % GROUP, part],
            dst_ref=recv1.at[g, part],
            send_sem=ssem1.at[c, s],
            recv_sem=rsem1.at[c, s],
            device_id=in_phase1(s),
            device_id_type=MESH,
        )

    def phase2(c, s):
        part = pl.ds(c * CHUNK, CHUNK)
        return pltpu.make_async_remote_copy(
            src_ref=send2.at[(h + s) % GROUP, part],
            dst_ref=recv2.at[h, part],
            send_sem=ssem2.at[c, s],
            recv_sem=rsem2.at[c, s],
            device_id=in_phase2(s),
            device_id_type=MESH,
        )

    def each(action):
        def one(s, carry):
            action(s)
            return carry

        lax.fori_loop(1, GROUP, one, 0)

    for c in range(CHUNKS):
        each(lambda s: phase1(c, s).start())
    recv1[g] = outg[g]

    for copy in inputs[2:5]:
        copy.wait()

    slots = fsrc[...]
    owner = slots >> 3
    from_g = (owner >> 5) * 2 + ((owner >> 1) & 1)
    from_h = ((owner >> 2) & 3) * 4 + ((owner >> 4) & 1) * 2 + (owner & 1)
    places = from_h * 128 + from_g * 8 + (slots & 7)
    low_places = places & 255
    sids[...] = places >> 8
    fsrc[...] = low_places
    links = nbr[...]
    layer = lax.broadcasted_iota(jnp.int32, (6, CELLS), 1) >> 9
    sidn[...] = jnp.where(links >= EXT, NEAR - 1, (links >> 8) - 2 * layer)

    def hot_start(c, carry):
        cells = pl.ds(pl.multiple_of(c * TILE, TILE), TILE)
        for side in range(2):
            ohs[side, c] = one_hot(fsrc[side : side + 1, cells])
        for k in range(6):
            ohn[k, c] = one_hot(nbr[k : k + 1, cells] & 255)
        return carry

    lax.fori_loop(0, TILES, hot_start, 0)
    near[:, 12 * SPLIT :, :] = jnp.zeros((2, 2 * SPLIT, TILE), BF16)
    sub = lax.broadcasted_iota(jnp.int32, (8, 128), 0)
    for k in range(6):
        for w in range(NV):
            column = jnp.zeros((8, 128), F32)
            for v in range(NV):
                column = jnp.where(sub == v, mix[v, k, w], column)
            mixcol[k, w] = column

    for c in range(CHUNKS):
        each(lambda s: phase1(c, s).wait_recv())
        for r in range(CHUNK // 8):
            part = pl.ds(c * CHUNK + 8 * r, 8)
            x = [recv1[j, part, :] for j in range(GROUP)]
            for bit in range(4):
                step = 8 << bit
                keep = (lane & step) == 0
                for a in range(GROUP):
                    b = a | (1 << bit)
                    if a != b:
                        low = jnp.where(keep, x[a], pltpu.roll(x[b], step, 1))
                        high = jnp.where(keep, pltpu.roll(x[a], 128 - step, 1), x[b])
                        x[a], x[b] = low, high
            for j in range(GROUP):
                send2[j, part, :] = x[j]
        each(lambda s: phase2(c, s).start())
    recv2[h] = send2[h]
    for c in range(CHUNKS):
        each(lambda s: phase2(c, s).wait_recv())

    for s in range(SOURCES):
        for side in range(2):
            high, low = halves(recv2[2 * s + side])
            rtab[s * SPLIT : s * SPLIT + ROWS, side * 128 : side * 128 + 128] = high
            rtab[s * SPLIT + ROWS : (s + 1) * SPLIT, side * 128 : side * 128 + 128] = low

    my_row = jnp.where(i == 0, RAD - 1, 0) * AXIAL

    def radial_copy(seg, a):
        return pltpu.make_async_remote_copy(
            src_ref=field.at[seg, :, lanes(RIM + a * RIM + my_row, AXIAL)],
            dst_ref=field.at[seg, :, lanes(EXT + a * AXIAL, AXIAL)],
            send_sem=hssem.at[seg, a],
            recv_sem=hrsem.at[seg, a],
            device_id=partner,
            device_id_type=MESH,
        )

    def behind_copy(seg):
        return pltpu.make_async_remote_copy(
            src_ref=field.at[seg, :, pl.ds(RIM, RIM)],
            dst_ref=field.at[seg, :, pl.ds(RIM + CELLS, RIM)],
            send_sem=hssem.at[seg, 4],
            recv_sem=hrsem.at[seg, 4],
            device_id=behind,
            device_id_type=MESH,
        )

    def ahead_copy(seg):
        return pltpu.make_async_remote_copy(
            src_ref=field.at[seg, :, pl.ds(CELLS, RIM)],
            dst_ref=field.at[seg, :, pl.ds(0, RIM)],
            send_sem=hssem.at[seg, 5],
            recv_sem=hrsem.at[seg, 5],
            device_id=ahead,
            device_id_type=MESH,
        )

    def send_layer(seg, j, a):
        radial_copy(seg, a).start()

        @pl.when(j == 2)
        def _():
            behind_copy(seg).start()

        @pl.when(j == 3)
        def _():
            ahead_copy(seg).start()

    def put(side, at, values):
        high, low = halves(jnp.concatenate(values, axis=0))
        near[side, pl.ds(pl.multiple_of(at * SPLIT, 16), ROWS), :] = high
        near[side, pl.ds(pl.multiple_of(at * SPLIT + ROWS, 16), ROWS), :] = low

    def layer_of(j):
        return jnp.where(j < 2, j + 1, (j - 2) * 3)

    for copy in inputs[5:]:
        copy.wait()

    def start_layer(j, carry):
        a = layer_of(j)
        for half in range(2):
            c = 2 * a + half
            cells = lanes(c * TILE, TILE)
            first = pick(rtab[...], ohs[0, c], sids[0:1, cells], SOURCES)
            second = pick(rtab[...], ohs[1, c], sids[1:2, cells], SOURCES)
            share = jnp.broadcast_to(weight[:, cells], (8, TILE))
            begin = [share * x + (1.0 - share) * y for x, y in zip(first, second)]
            for r in range(ROWS // 8):
                field[0, 8 * r : 8 * r + 8, lanes(RIM + c * TILE, TILE)] = begin[r]
            put(0, 2 + c, begin)
        send_layer(0, j, a)
        return carry

    lax.fori_loop(0, LAYERS, start_layer, 0)

    omega = freq[0]

    def rate_layer(at, carry):
        seg = at // LAYERS
        side = seg % 2
        j = at % LAYERS
        a = layer_of(j)

        def arrived(start, at_set):
            for half in range(2):
                put(side, at_set + half, [field[seg, :, start + half * TILE : start + (half + 1) * TILE]])

        @pl.when(j == 2)
        def _():
            ahead_copy(seg).wait_recv()
            arrived(0, 0)

        @pl.when(j == 3)
        def _():
            behind_copy(seg).wait_recv()
            arrived(RIM + CELLS, 10)

        radial_copy(seg, a).wait_recv()
        high, low = halves(field[seg, :, lanes(EXT + a * AXIAL, AXIAL)])
        across = (12 + a // 2) * SPLIT
        column = lanes(a % 2 * AXIAL, AXIAL)
        near[side, pl.ds(pl.multiple_of(across, 16), ROWS), column] = high
        near[side, pl.ds(pl.multiple_of(across + ROWS, 16), ROWS), column] = low

        coef = jnp.where(seg == 2, SEGMENT_COEFS[2], SEGMENT_COEFS[0])
        for half in range(2):
            c = 2 * a + half
            cells = lanes(c * TILE, TILE)
            here = lanes(RIM + c * TILE, TILE)
            own = [field[seg, 8 * r : 8 * r + 8, here] for r in range(ROWS // 8)]
            mine = near[side, pl.ds(pl.multiple_of((2 + c) * SPLIT, 16), SPLIT), :]
            turned = jnp.dot(dmat[...], mine, preferred_element_type=F32)
            rate = [omega * (turned[8 * r : 8 * r + 8] + turned[ROWS + 8 * r : ROWS + 8 * r + 8]) for r in range(ROWS // 8)]
            table = jnp.concatenate(
                [
                    near[side, pl.ds(pl.multiple_of(2 * a * SPLIT, 16), 6 * SPLIT), :],
                    near[side, pl.ds(pl.multiple_of(across, 16), SPLIT), :],
                ],
                axis=0,
            )
            for k in range(6):
                found = pick(table, ohn[k, c], sidn[k : k + 1, cells], NEAR)
                face = jnp.broadcast_to(area[k : k + 1, cells], (8, TILE))
                jump = [(found[r] - own[r]) * face for r in range(ROWS // 8)]
                for v in range(NV):
                    flux = mix[v, k, 0] * jump[0]
                    for w in range(1, NV):
                        flux = flux + mix[v, k, w] * jump[w]
                    rate[v] = rate[v] - flux
                last = jnp.zeros((8, TILE), F32)
                for w in range(NV):
                    column = mixcol[k, w]
                    last = last + jnp.concatenate([column, column], axis=1) * jnp.broadcast_to(jump[NV][w : w + 1], (8, TILE))
                rate[NV] = rate[NV] - last
            step = jnp.broadcast_to(coef * dt[:, cells], (8, TILE))
            after = [field[0, 8 * r : 8 * r + 8, here] - step * rate[r] for r in range(ROWS // 8)]
            for r in range(ROWS // 8):
                field[seg + 1, 8 * r : 8 * r + 8, here] = after[r]
            put(1 - side, 2 + c, after)

        @pl.when(seg < 2)
        def _():
            send_layer(seg + 1, j, a)

        return carry

    lax.fori_loop(0, 3 * LAYERS, rate_layer, 0)

    for v in range(NV):
        out[0:8, v, :] = field[3, 8 * v : 8 * v + 8, RIM : RIM + CELLS]
    out[8] = field[3, 8 * NV : 9 * NV, RIM : RIM + CELLS]

    for c in range(CHUNKS):
        each(lambda s: phase1(c, s).wait_send())
        each(lambda s: phase2(c, s).wait_send())
    for seg in range(3):
        for a in range(LAYERS):
            radial_copy(seg, a).wait_send()
        behind_copy(seg).wait_send()
        ahead_copy(seg).wait_send()


def per_device(coarse_state, send_cells, fine_source, weight, neighbours, face_area, time_step, mixing, frequency):
    vmem = pl.BlockSpec(memory_space=pltpu.VMEM)
    hbm = pl.BlockSpec(memory_space=pltpu.HBM)
    fine = pl.pallas_call(
        kernel,
        out_shape=jax.ShapeDtypeStruct((NI, NV, CELLS), F32),
        in_specs=[hbm] * 10,
        out_specs=vmem,
        scratch_shapes=[
            pltpu.VMEM((NI, NV, TILE), F32),
            pltpu.VMEM((1, CELLS), jnp.int32),
            pltpu.VMEM((2, CELLS), jnp.int32),
            pltpu.VMEM((1, CELLS), F32),
            pltpu.VMEM((6, CELLS), jnp.int32),
            pltpu.VMEM((6, CELLS), F32),
            pltpu.VMEM((1, CELLS), F32),
            pltpu.SMEM((NV, 6, NV), F32),
            pltpu.SMEM((1,), F32),
            pltpu.VMEM((SPLIT, SPLIT), BF16),
            pltpu.SemaphoreType.DMA((10,)),
            pltpu.VMEM((GROUP, ROWS, 128), F32),
            pltpu.VMEM((GROUP, ROWS, 128), F32),
            pltpu.VMEM((GROUP, ROWS, 128), F32),
            pltpu.VMEM((GROUP, ROWS, 128), F32),
            pltpu.VMEM((SOURCES * SPLIT, TILE), BF16),
            pltpu.VMEM((2, TILES, TILE, TILE), BF16),
            pltpu.VMEM((6, TILES, TILE, TILE), BF16),
            pltpu.VMEM((2, 14 * SPLIT, TILE), BF16),
            pltpu.VMEM((6, CELLS), jnp.int32),
            pltpu.VMEM((2, CELLS), jnp.int32),
            pltpu.VMEM((4, ROWS, CELLS + 3 * RIM), F32),
            pltpu.VMEM((6, NV, 8, 128), F32),
            pltpu.SemaphoreType.DMA((CHUNKS, GROUP)),
            pltpu.SemaphoreType.DMA((CHUNKS, GROUP)),
            pltpu.SemaphoreType.DMA((CHUNKS, GROUP)),
            pltpu.SemaphoreType.DMA((CHUNKS, GROUP)),
            pltpu.SemaphoreType.DMA((3, 6)),
            pltpu.SemaphoreType.DMA((3, 6)),
        ],
        compiler_params=pltpu.CompilerParams(
            collective_id=0, has_side_effects=True, vmem_limit_bytes=48 * 2**20
        ),
        name="grid_sequence",
    )(
        *[
            x if x.shape == (1,) else pltpu.with_memory_space_constraint(x, pltpu.HBM)
            for x in (
                coarse_state.transpose(1, 0, 2),
                send_cells,
                fine_source,
                weight.reshape(1, CELLS),
                neighbours,
                face_area,
                time_step.reshape(1, CELLS),
                mixing.transpose(1, 0, 2),
                frequency,
                jnp.asarray(spectral_rows()),
            )
        ]
    )
    return fine.transpose(1, 0, 2)


def solution(mesh):
    placed = (
        P(None, None, ("theta", "inst")),
        P(("theta", "inst"), None),
        P(None, ("theta", "inst")),
        P(("theta", "inst")),
        P(None, ("theta", "inst")),
        P(None, ("theta", "inst")),
        P(("theta", "inst")),
        P(),
        P(),
    )
    return jax.shard_map(
        per_device,
        mesh=mesh,
        in_specs=placed,
        out_specs=P(None, None, ("theta", "inst")),
        check_vma=False,
    )
```

```python
import functools

import jax
import jax.numpy as jnp
import numpy as np
from jax import lax
from jax.experimental import pallas as pl
from jax.experimental.pallas import tpu as pltpu
from jax.sharding import PartitionSpec as P

NV = 5
NI = 9
AXIAL = 128
RAD = 4
LAYERS = 4
RIM = 512
CELLS = 2048
EXT = CELLS + 2 * RIM
ROWS = 48
SPLIT = 2 * ROWS
TILE = 256
TILES = CELLS // TILE
NEAR = 7
NEAR_BLOCKS = 13
TOGETHER = 1
BY_LANES = {}
GROUP = 16
CHUNK = 24
CHUNKS = ROWS // CHUNK
SOURCES = 8

SEGMENT_COEFS = (0.6, 0.6, 1.0)
MESH = pl.DeviceIdType.MESH
F32 = jnp.float32
BF16 = jnp.bfloat16


def spectral_rows():
    offsets = np.arange(NI)[:, None] - np.arange(NI)[None, :]
    sine = np.where(offsets == 0, 1.0, np.sin(np.pi * offsets / NI))
    matrix = np.where(offsets == 0, 0.0, 0.5 * np.where(offsets % 2 == 0, 1.0, -1.0) / sine)
    place = np.array([[v * 8 + n if n < 8 else NV * 8 + v for n in range(NI)] for v in range(NV)])
    full = np.zeros((ROWS, ROWS), np.float32)
    for v in range(NV):
        full[np.ix_(place[v], place[v])] = matrix
    high = full.astype(BF16)
    low = (full - high.astype(np.float32)).astype(BF16)
    return np.concatenate([np.concatenate([high, high], 1), np.concatenate([low, low], 1)], 0)


def halves(x):
    high = x.astype(BF16)
    return high, (x - high.astype(F32)).astype(BF16)


def one_hot(low):
    hit = lax.broadcasted_iota(jnp.int32, (TILE, TILE), 0) == low
    return jnp.where(hit, 1.0, 0.0).astype(BF16)


def pick(table, hot, sets, count):
    found = jnp.dot(table, hot, preferred_element_type=F32)
    sets = jnp.broadcast_to(sets, (8, TILE))
    masks = [sets == s for s in range(1, count)]
    rows = []
    for r in range(0, ROWS, 8):
        parts = []
        for base in (r, ROWS + r):
            value = found[base : base + 8]
            for s in range(1, count):
                value = jnp.where(masks[s - 1], found[s * SPLIT + base : s * SPLIT + base + 8], value)
            parts.append(value)
        rows.append(parts[0] + parts[1])
    return rows


def turn_lanes(blocks, place, sets):
    columns = []
    for at in range(0, TILE, 128):
        lane = jnp.broadcast_to(place[:, at : at + 128], (8, 128))
        block = jnp.broadcast_to(sets[:, at : at + 128], (8, 128))
        masks = [block == s for s in range(1, NEAR_BLOCKS)]
        rows = []
        for r in range(ROWS // 8):
            value = jnp.take_along_axis(blocks(0, r), lane, axis=1, mode="promise_in_bounds")
            for s in range(1, NEAR_BLOCKS):
                found = jnp.take_along_axis(blocks(s, r), lane, axis=1, mode="promise_in_bounds")
                value = jnp.where(masks[s - 1], found, value)
            rows.append(value)
        columns.append(rows)
    return [jnp.concatenate([x, y], axis=1) for x, y in zip(*columns)]


def kernel(
    coarse_in, send_in, fsrc_in, weight_in, nbr_in, area_in, dt_in, mix_in, freq_in, dmat_in, out,
    coarse, send, fsrc, weight, nbr, area, dt, mix, freq, dmat, isem, outg, recv1, send2, recv2, rtab, ohs, ohn, near0, near1, sidn, sids, field0, field1, field2, field3, mixcol,
    ssem1, rsem1, ssem2, rsem2, hssem, hrsem,
):
    inputs = [
        pltpu.make_async_copy(src, dst, isem.at[at])
        for at, (src, dst) in enumerate(
            [
                (coarse_in, coarse), (send_in, send), (fsrc_in, fsrc), (nbr_in, nbr), (mix_in, mix),
                (freq_in, freq), (weight_in, weight), (area_in, area), (dt_in, dt), (dmat_in, dmat),
            ]
        )
    ]
    for copy in inputs:
        copy.start()

    field = [field0, field1, field2, field3]
    near = [near0, near1]
    t = lax.axis_index("theta")
    i = lax.axis_index("inst")
    count = 128
    z, x_lo, y, core = t // 16, t // 8 % 2, t // 2 % 4, t % 2
    g = z * 2 + core
    h = y * 4 + x_lo * 2 + i

    def in_phase1(s):
        other = (g + s) % GROUP
        return ((other // 2 * 2 + x_lo) * 4 + y) * 2 + other % 2, i

    def in_phase2(s):
        other = (h + s) % GROUP
        return ((z * 2 + other // 2 % 2) * 4 + other // 4) * 2 + core, other % 2

    ahead = ((t + 1) % count, i)
    behind = ((t + count - 1) % count, i)
    partner = (t, 1 - i)

    def lanes(start, size):
        return pl.ds(pl.multiple_of(start, 128), size)

    barrier = pltpu.get_barrier_semaphore()

    def greet(s, carry):
        pl.semaphore_signal(barrier, inc=1, device_id=in_phase1(s), device_id_type=MESH)
        pl.semaphore_signal(barrier, inc=1, device_id=in_phase2(s), device_id_type=MESH)
        return carry

    lax.fori_loop(1, GROUP, greet, 0)
    pl.semaphore_signal(barrier, inc=1, device_id=ahead, device_id_type=MESH)
    pl.semaphore_signal(barrier, inc=1, device_id=behind, device_id_type=MESH)

    inputs[0].wait()
    inputs[1].wait()

    rows = jnp.concatenate(
        [coarse[0:8, v, :] for v in range(NV)] + [coarse[8], jnp.zeros((ROWS - NV * NI, TILE), F32)], axis=0
    )
    table = jnp.concatenate(halves(rows), axis=0)

    lane = lax.broadcasted_iota(jnp.int32, (8, 128), 1)

    def gather_out(c, carry):
        even = send[:, lanes(c * TILE, 128)]
        odd = send[:, lanes(c * TILE + 128, 128)]
        keep = (lane[:1] & 16) == 0
        first = jnp.where(keep, even, pltpu.roll(odd, 16, 1))
        second = jnp.where(keep, pltpu.roll(even, 112, 1), odd)
        low = jnp.maximum(jnp.concatenate([first, second], axis=1), 0)
        found = jnp.dot(table, one_hot(low), preferred_element_type=F32)
        found = found[:ROWS] + found[ROWS:]
        outg[2 * c] = found[:, :128]
        outg[2 * c + 1] = found[:, 128:]
        return carry

    lax.fori_loop(0, TILES, gather_out, 0)

    pl.semaphore_wait(barrier, 2 * (GROUP - 1) + 2)

    def phase1(c, s):
        part = pl.ds(c * CHUNK, CHUNK)
        return pltpu.make_async_remote_copy(
            src_ref=outg.at[(g + s) % GROUP, part],
            dst_ref=recv1.at[g, part],
            send_sem=ssem1.at[c, s],
            recv_sem=rsem1.at[c, s],
            device_id=in_phase1(s),
            device_id_type=MESH,
        )

    def phase2(c, s):
        part = pl.ds(c * CHUNK, CHUNK)
        return pltpu.make_async_remote_copy(
            src_ref=send2.at[(h + s) % GROUP, part],
            dst_ref=recv2.at[h, part],
            send_sem=ssem2.at[c, s],
            recv_sem=rsem2.at[c, s],
            device_id=in_phase2(s),
            device_id_type=MESH,
        )

    def each(action):
        for s in range(1, GROUP):
            action(s)

    for c in range(CHUNKS):
        each(lambda s: phase1(c, s).start())
    recv1[g] = outg[g]

    for copy in inputs[2:5]:
        copy.wait()

    slots = fsrc[...]
    owner = slots >> 3
    from_g = (owner >> 5) * 2 + ((owner >> 1) & 1)
    from_h = ((owner >> 2) & 3) * 4 + ((owner >> 4) & 1) * 2 + (owner & 1)
    places = from_h * 128 + from_g * 8 + (slots & 7)
    low_places = places & 255
    sids[...] = places >> 8
    fsrc[...] = low_places
    links = nbr[...]
    layer = lax.broadcasted_iota(jnp.int32, (6, CELLS), 1) >> 9
    sidn[...] = jnp.where(links >= EXT, NEAR - 1, (links >> 8) - 2 * layer)

    def hot_start(c, carry):
        cells = pl.ds(pl.multiple_of(c * TILE, TILE), TILE)
        for side in range(2):
            ohs[side, c] = one_hot(fsrc[side : side + 1, cells])
        for k in range(6):
            ohn[k, c] = one_hot(nbr[k : k + 1, cells] & 255)
        return carry

    lax.fori_loop(0, TILES, hot_start, 0)
    for table_ref in near:
        table_ref[12 * SPLIT :, :] = jnp.zeros((2 * SPLIT, TILE), BF16)
    sub = lax.broadcasted_iota(jnp.int32, (8, 128), 0)
    for k in range(6):
        for w in range(NV):
            column = jnp.zeros((8, 128), F32)
            for v in range(NV):
                column = jnp.where(sub == v, mix[v, k, w], column)
            mixcol[k, w] = column

    for c in range(CHUNKS):
        each(lambda s: phase1(c, s).wait_recv())
        for r in range(CHUNK // 8):
            part = pl.ds(c * CHUNK + 8 * r, 8)
            x = [recv1[j, part, :] for j in range(GROUP)]
            for bit in range(4):
                step = 8 << bit
                keep = (lane & step) == 0
                for a in range(GROUP):
                    b = a | (1 << bit)
                    if a != b:
                        low = jnp.where(keep, x[a], pltpu.roll(x[b], step, 1))
                        high = jnp.where(keep, pltpu.roll(x[a], 128 - step, 1), x[b])
                        x[a], x[b] = low, high
            for j in range(GROUP):
                send2[j, part, :] = x[j]
        each(lambda s: phase2(c, s).start())
    recv2[h] = send2[h]
    for c in range(CHUNKS):
        each(lambda s: phase2(c, s).wait_recv())

    for s in range(SOURCES):
        for side in range(2):
            high, low = halves(recv2[2 * s + side])
            rtab[s * SPLIT : s * SPLIT + ROWS, side * 128 : side * 128 + 128] = high
            rtab[s * SPLIT + ROWS : (s + 1) * SPLIT, side * 128 : side * 128 + 128] = low

    my_row = jnp.where(i == 0, RAD - 1, 0) * AXIAL

    def radial_copy(seg, a):
        return pltpu.make_async_remote_copy(
            src_ref=field[seg].at[:, lanes(RIM + a * RIM + my_row, AXIAL)],
            dst_ref=field[seg].at[:, lanes(EXT + a * AXIAL, AXIAL)],
            send_sem=hssem.at[seg, a],
            recv_sem=hrsem.at[seg, a],
            device_id=partner,
            device_id_type=MESH,
        )

    def behind_copy(seg):
        return pltpu.make_async_remote_copy(
            src_ref=field[seg].at[:, pl.ds(RIM, RIM)],
            dst_ref=field[seg].at[:, pl.ds(RIM + CELLS, RIM)],
            send_sem=hssem.at[seg, 4],
            recv_sem=hrsem.at[seg, 4],
            device_id=behind,
            device_id_type=MESH,
        )

    def ahead_copy(seg):
        return pltpu.make_async_remote_copy(
            src_ref=field[seg].at[:, pl.ds(CELLS, RIM)],
            dst_ref=field[seg].at[:, pl.ds(0, RIM)],
            send_sem=hssem.at[seg, 5],
            recv_sem=hrsem.at[seg, 5],
            device_id=ahead,
            device_id_type=MESH,
        )

    def send_layer(seg, j, a):
        radial_copy(seg, a).start()

        @pl.when(j == 2)
        def _():
            behind_copy(seg).start()

        @pl.when(j == 3)
        def _():
            ahead_copy(seg).start()

    def put(side, at, values):
        high, low = halves(jnp.concatenate(values, axis=0))
        near[side][pl.ds(pl.multiple_of(at * SPLIT, 16), ROWS), :] = high
        near[side][pl.ds(pl.multiple_of(at * SPLIT + ROWS, 16), ROWS), :] = low

    def layer_of(j):
        return jnp.where(j < 2, j + 1, (j - 2) * 3)

    for copy in inputs[5:]:
        copy.wait()

    def start_layer(j, carry):
        a = layer_of(j)
        for half in range(2):
            c = 2 * a + half
            cells = lanes(c * TILE, TILE)
            first = pick(rtab[...], ohs[0, c], sids[0:1, cells], SOURCES)
            second = pick(rtab[...], ohs[1, c], sids[1:2, cells], SOURCES)
            share = jnp.broadcast_to(weight[:, cells], (8, TILE))
            begin = [share * x + (1.0 - share) * y for x, y in zip(first, second)]
            for r in range(ROWS // 8):
                field[0][8 * r : 8 * r + 8, lanes(RIM + c * TILE, TILE)] = begin[r]
            put(0, 2 + c, begin)
        send_layer(0, j, a)
        return carry

    lax.fori_loop(0, LAYERS, start_layer, 0)

    omega = freq[0]

    def rate_tile(seg, side, coef, a, half):
        c = 2 * a + half
        cells = lanes(c * TILE, TILE)
        here = lanes(RIM + c * TILE, TILE)
        across = (12 + a // 2) * SPLIT
        own = [field[seg][8 * r : 8 * r + 8, here] for r in range(ROWS // 8)]
        mine = near[side][pl.ds(pl.multiple_of((2 + c) * SPLIT, 16), SPLIT), :]
        turned = jnp.dot(dmat[...], mine, preferred_element_type=F32)
        rate = [omega * (turned[8 * r : 8 * r + 8] + turned[ROWS + 8 * r : ROWS + 8 * r + 8]) for r in range(ROWS // 8)]
        table = jnp.concatenate(
            [
                near[side][pl.ds(pl.multiple_of(2 * a * SPLIT, 16), 6 * SPLIT), :],
                near[side][pl.ds(pl.multiple_of(across, 16), SPLIT), :],
            ],
            axis=0,
        )

        def block(s, r):
            start = EXT + a * AXIAL if s == NEAR_BLOCKS - 1 else a * RIM + s * 128
            return field[seg][8 * r : 8 * r + 8, lanes(start, 128)]

        for k in range(6):
            if (half, k) in BY_LANES:
                links = nbr[k : k + 1, cells]
                sets = jnp.where(links >= EXT, NEAR_BLOCKS - 1, (links >> 7) - 4 * a)
                found = turn_lanes(block, links & 127, sets)
            else:
                found = pick(table, ohn[k, c], sidn[k : k + 1, cells], NEAR)
            face = jnp.broadcast_to(area[k : k + 1, cells], (8, TILE))
            jump = [(found[r] - own[r]) * face for r in range(ROWS // 8)]
            for v in range(NV):
                flux = mix[v, k, 0] * jump[0]
                for w in range(1, NV):
                    flux = flux + mix[v, k, w] * jump[w]
                rate[v] = rate[v] - flux
            last = jnp.zeros((8, TILE), F32)
            for w in range(NV):
                column = mixcol[k, w]
                last = last + jnp.concatenate([column, column], axis=1) * jnp.broadcast_to(jump[NV][w : w + 1], (8, TILE))
            rate[NV] = rate[NV] - last
        step = jnp.broadcast_to(coef * dt[:, cells], (8, TILE))
        after = [field[0][8 * r : 8 * r + 8, here] - step * rate[r] for r in range(ROWS // 8)]
        for r in range(ROWS // 8):
            field[seg + 1][8 * r : 8 * r + 8, here] = after[r]
        if seg < 2:
            put(1 - side, 2 + c, after)

    def rate_layers(seg, step_at):
        side = seg % 2
        coef = SEGMENT_COEFS[seg]
        group = [layer_of(step_at * TOGETHER + n) for n in range(TOGETHER)]

        def arrived(start, at_set):
            for half in range(2):
                put(side, at_set + half, [field[seg][:, start + half * TILE : start + (half + 1) * TILE]])

        for n in range(TOGETHER):

            @pl.when(step_at * TOGETHER + n == 2)
            def _():
                ahead_copy(seg).wait_recv()
                arrived(0, 0)

            @pl.when(step_at * TOGETHER + n == 3)
            def _():
                behind_copy(seg).wait_recv()
                arrived(RIM + CELLS, 10)

        for a in group:
            radial_copy(seg, a).wait_recv()
            high, low = halves(field[seg][:, lanes(EXT + a * AXIAL, AXIAL)])
            across = (12 + a // 2) * SPLIT
            column = lanes(a % 2 * AXIAL, AXIAL)
            near[side][pl.ds(pl.multiple_of(across, 16), ROWS), column] = high
            near[side][pl.ds(pl.multiple_of(across + ROWS, 16), ROWS), column] = low

        for a in group:
            for half in range(2):
                rate_tile(seg, side, coef, a, half)

        if seg < 2:
            for n in range(TOGETHER):
                send_layer(seg + 1, step_at * TOGETHER + n, group[n])

    for seg in range(3):

        def rate_step(step_at, carry):
            rate_layers(seg, step_at)
            return carry

        lax.fori_loop(0, LAYERS // TOGETHER, rate_step, 0)

    for v in range(NV):
        out[0:8, v, :] = field[3][8 * v : 8 * v + 8, RIM : RIM + CELLS]
    out[8] = field[3][8 * NV : 9 * NV, RIM : RIM + CELLS]

    for c in range(CHUNKS):
        each(lambda s: phase1(c, s).wait_send())
        each(lambda s: phase2(c, s).wait_send())
    for seg in range(3):
        for a in range(LAYERS):
            radial_copy(seg, a).wait_send()
        behind_copy(seg).wait_send()
        ahead_copy(seg).wait_send()


def per_device(coarse_state, send_cells, fine_source, weight, neighbours, face_area, time_step, mixing, frequency):
    vmem = pl.BlockSpec(memory_space=pltpu.VMEM)
    hbm = pl.BlockSpec(memory_space=pltpu.HBM)
    fine = pl.pallas_call(
        kernel,
        out_shape=jax.ShapeDtypeStruct((NI, NV, CELLS), F32),
        in_specs=[hbm] * 10,
        out_specs=vmem,
        scratch_shapes=[
            pltpu.VMEM((NI, NV, TILE), F32),
            pltpu.VMEM((1, CELLS), jnp.int32),
            pltpu.VMEM((2, CELLS), jnp.int32),
            pltpu.VMEM((1, CELLS), F32),
            pltpu.VMEM((6, CELLS), jnp.int32),
            pltpu.VMEM((6, CELLS), F32),
            pltpu.VMEM((1, CELLS), F32),
            pltpu.SMEM((NV, 6, NV), F32),
            pltpu.SMEM((1,), F32),
            pltpu.VMEM((SPLIT, SPLIT), BF16),
            pltpu.SemaphoreType.DMA((10,)),
            pltpu.VMEM((GROUP, ROWS, 128), F32),
            pltpu.VMEM((GROUP, ROWS, 128), F32),
            pltpu.VMEM((GROUP, ROWS, 128), F32),
            pltpu.VMEM((GROUP, ROWS, 128), F32),
            pltpu.VMEM((SOURCES * SPLIT, TILE), BF16),
            pltpu.VMEM((2, TILES, TILE, TILE), BF16),
            pltpu.VMEM((6, TILES, TILE, TILE), BF16),
            pltpu.VMEM((14 * SPLIT, TILE), BF16),
            pltpu.VMEM((14 * SPLIT, TILE), BF16),
            pltpu.VMEM((6, CELLS), jnp.int32),
            pltpu.VMEM((2, CELLS), jnp.int32),
            pltpu.VMEM((ROWS, CELLS + 3 * RIM), F32),
            pltpu.VMEM((ROWS, CELLS + 3 * RIM), F32),
            pltpu.VMEM((ROWS, CELLS + 3 * RIM), F32),
            pltpu.VMEM((ROWS, CELLS + 3 * RIM), F32),
            pltpu.VMEM((6, NV, 8, 128), F32),
            pltpu.SemaphoreType.DMA((CHUNKS, GROUP)),
            pltpu.SemaphoreType.DMA((CHUNKS, GROUP)),
            pltpu.SemaphoreType.DMA((CHUNKS, GROUP)),
            pltpu.SemaphoreType.DMA((CHUNKS, GROUP)),
            pltpu.SemaphoreType.DMA((3, 6)),
            pltpu.SemaphoreType.DMA((3, 6)),
        ],
        compiler_params=pltpu.CompilerParams(
            collective_id=0, has_side_effects=True, vmem_limit_bytes=48 * 2**20
        ),
        name="grid_sequence",
    )(
        *[
            x if x.shape == (1,) else pltpu.with_memory_space_constraint(x, pltpu.HBM)
            for x in (
                coarse_state.transpose(1, 0, 2),
                send_cells,
                fine_source,
                weight.reshape(1, CELLS),
                neighbours,
                face_area,
                time_step.reshape(1, CELLS),
                mixing.transpose(1, 0, 2),
                frequency,
                jnp.asarray(spectral_rows()),
            )
        ]
    )
    return fine.transpose(1, 0, 2)


def solution(mesh):
    placed = (
        P(None, None, ("theta", "inst")),
        P(("theta", "inst"), None),
        P(None, ("theta", "inst")),
        P(("theta", "inst")),
        P(None, ("theta", "inst")),
        P(None, ("theta", "inst")),
        P(("theta", "inst")),
        P(),
        P(),
    )
    return jax.shard_map(
        per_device,
        mesh=mesh,
        in_specs=placed,
        out_specs=P(None, None, ("theta", "inst")),
        check_vma=False,
    )
```

```python
import functools

import jax
import jax.numpy as jnp
import numpy as np
from jax import lax
from jax.experimental import pallas as pl
from jax.experimental.pallas import tpu as pltpu
from jax.sharding import PartitionSpec as P

NV = 5
NI = 9
AXIAL = 128
RAD = 4
LAYERS = 4
RIM = 512
CELLS = 2048
EXT = CELLS + 2 * RIM
ROWS = 48
SPLIT = 2 * ROWS
TILE = 256
TILES = CELLS // TILE
NEAR = 7
NEAR_BLOCKS = 13
TOGETHER = 1
BY_MATRIX = 5
GROUP = 16
CHUNK = 24
CHUNKS = ROWS // CHUNK
SOURCES = 8

SEGMENT_COEFS = (0.6, 0.6, 1.0)
MESH = pl.DeviceIdType.MESH
F32 = jnp.float32
BF16 = jnp.bfloat16


def spectral_rows():
    offsets = np.arange(NI)[:, None] - np.arange(NI)[None, :]
    sine = np.where(offsets == 0, 1.0, np.sin(np.pi * offsets / NI))
    matrix = np.where(offsets == 0, 0.0, 0.5 * np.where(offsets % 2 == 0, 1.0, -1.0) / sine)
    place = np.array([[v * 8 + n if n < 8 else NV * 8 + v for n in range(NI)] for v in range(NV)])
    full = np.zeros((ROWS, ROWS), np.float32)
    for v in range(NV):
        full[np.ix_(place[v], place[v])] = matrix
    high = full.astype(BF16)
    low = (full - high.astype(np.float32)).astype(BF16)
    twice = [np.concatenate([x[:, r : r + 16]] * 2, 1) for x in (high, low) for r in range(0, ROWS, 16)]
    return np.concatenate([np.concatenate(twice[:3], 1), np.concatenate(twice[3:], 1)], 0)


def halves(x):
    high = x.astype(BF16)
    return high, (x - high.astype(F32)).astype(BF16)


def one_hot(low):
    hit = lax.broadcasted_iota(jnp.int32, (TILE, TILE), 0) == low
    return jnp.where(hit, 1.0, 0.0).astype(BF16)


def pick(table, hot, sets, count):
    found = jnp.dot(table, hot, preferred_element_type=F32)
    sets = jnp.broadcast_to(sets, (8, TILE))
    masks = [sets == s for s in range(1, count)]
    rows = []
    for r in range(0, ROWS, 8):
        parts = []
        for half in range(2):
            base = ((r // 16) * 2 + half) * count * 16 + r % 16
            value = found[base : base + 8]
            for s in range(1, count):
                value = jnp.where(masks[s - 1], found[base + s * 16 : base + s * 16 + 8], value)
            parts.append(value)
        rows.append(parts[0] + parts[1])
    return rows


def from_block(block, place, masks, values):
    merged = []
    for r in range(ROWS // 8):
        rows = block(r)
        found = [
            jnp.take_along_axis(rows, jnp.broadcast_to(place[:, at : at + 128], (8, 128)), axis=1, mode="promise_in_bounds")
            for at in range(0, TILE, 128)
        ]
        merged.append(jnp.where(masks, jnp.concatenate(found, axis=1), values[r]))
    return merged


def kernel(
    coarse_in, send_in, fsrc_in, weight_in, nbr_in, area_in, dt_in, mix_in, freq_in, dmat_in, out,
    coarse, send, fsrc, weight, nbr, area, dt, mix, freq, dmat, isem, outg, recv1, send2, recv2, rtab, ohs, ohn, near0, near1, sidn, sids, field0, field1, field2, field3, mixcol,
    ssem1, rsem1, ssem2, rsem2, hssem, hrsem,
):
    inputs = [
        pltpu.make_async_copy(src, dst, isem.at[at])
        for at, (src, dst) in enumerate(
            [
                (coarse_in, coarse), (send_in, send), (fsrc_in, fsrc), (nbr_in, nbr), (mix_in, mix),
                (freq_in, freq), (weight_in, weight), (area_in, area), (dt_in, dt), (dmat_in, dmat),
            ]
        )
    ]
    for copy in inputs:
        copy.start()

    field = [field0, field1, field2, field3]
    near = [near0, near1]
    t = lax.axis_index("theta")
    i = lax.axis_index("inst")
    count = 128
    z, x_lo, y, core = t // 16, t // 8 % 2, t // 2 % 4, t % 2
    g = z * 2 + core
    h = y * 4 + x_lo * 2 + i

    def in_phase1(s):
        other = (g + s) % GROUP
        return ((other // 2 * 2 + x_lo) * 4 + y) * 2 + other % 2, i

    def in_phase2(s):
        other = (h + s) % GROUP
        return ((z * 2 + other // 2 % 2) * 4 + other // 4) * 2 + core, other % 2

    ahead = ((t + 1) % count, i)
    behind = ((t + count - 1) % count, i)
    partner = (t, 1 - i)

    def lanes(start, size):
        return pl.ds(pl.multiple_of(start, 128), size)

    barrier = pltpu.get_barrier_semaphore()

    def greet(s, carry):
        pl.semaphore_signal(barrier, inc=1, device_id=in_phase1(s), device_id_type=MESH)
        pl.semaphore_signal(barrier, inc=1, device_id=in_phase2(s), device_id_type=MESH)
        return carry

    lax.fori_loop(1, GROUP, greet, 0)
    pl.semaphore_signal(barrier, inc=1, device_id=ahead, device_id_type=MESH)
    pl.semaphore_signal(barrier, inc=1, device_id=behind, device_id_type=MESH)

    inputs[0].wait()
    inputs[1].wait()

    rows = jnp.concatenate(
        [coarse[0:8, v, :] for v in range(NV)] + [coarse[8], jnp.zeros((ROWS - NV * NI, TILE), F32)], axis=0
    )
    table = jnp.concatenate(halves(rows), axis=0)

    lane = lax.broadcasted_iota(jnp.int32, (8, 128), 1)

    def gather_out(c, carry):
        even = send[:, lanes(c * TILE, 128)]
        odd = send[:, lanes(c * TILE + 128, 128)]
        keep = (lane[:1] & 16) == 0
        first = jnp.where(keep, even, pltpu.roll(odd, 16, 1))
        second = jnp.where(keep, pltpu.roll(even, 112, 1), odd)
        low = jnp.maximum(jnp.concatenate([first, second], axis=1), 0)
        found = jnp.dot(table, one_hot(low), preferred_element_type=F32)
        found = found[:ROWS] + found[ROWS:]
        outg[2 * c] = found[:, :128]
        outg[2 * c + 1] = found[:, 128:]
        return carry

    lax.fori_loop(0, TILES, gather_out, 0)

    pl.semaphore_wait(barrier, 2 * (GROUP - 1) + 2)

    def phase1(c, s):
        part = pl.ds(c * CHUNK, CHUNK)
        return pltpu.make_async_remote_copy(
            src_ref=outg.at[(g + s) % GROUP, part],
            dst_ref=recv1.at[g, part],
            send_sem=ssem1.at[c, s],
            recv_sem=rsem1.at[c, s],
            device_id=in_phase1(s),
            device_id_type=MESH,
        )

    def phase2(c, s):
        part = pl.ds(c * CHUNK, CHUNK)
        return pltpu.make_async_remote_copy(
            src_ref=send2.at[(h + s) % GROUP, part],
            dst_ref=recv2.at[h, part],
            send_sem=ssem2.at[c, s],
            recv_sem=rsem2.at[c, s],
            device_id=in_phase2(s),
            device_id_type=MESH,
        )

    def each(action):
        for s in range(1, GROUP):
            action(s)

    for c in range(CHUNKS):
        each(lambda s: phase1(c, s).start())
    recv1[g] = outg[g]

    for copy in inputs[2:5]:
        copy.wait()

    slots = fsrc[...]
    owner = slots >> 3
    from_g = (owner >> 5) * 2 + ((owner >> 1) & 1)
    from_h = ((owner >> 2) & 3) * 4 + ((owner >> 4) & 1) * 2 + (owner & 1)
    places = from_h * 128 + from_g * 8 + (slots & 7)
    low_places = places & 255
    sids[...] = places >> 8
    fsrc[...] = low_places
    links = nbr[...]
    layer = lax.broadcasted_iota(jnp.int32, (6, CELLS), 1) >> 9
    sidn[...] = jnp.where(links >= EXT, NEAR - 1, (links >> 8) - 2 * layer)

    def hot_start(c, carry):
        cells = pl.ds(pl.multiple_of(c * TILE, TILE), TILE)
        for side in range(2):
            ohs[side, c] = one_hot(fsrc[side : side + 1, cells])
        for k in range(6):
            ohn[k, c] = one_hot(nbr[k : k + 1, cells] & 255)
        return carry

    lax.fori_loop(0, TILES, hot_start, 0)
    sub = lax.broadcasted_iota(jnp.int32, (8, 128), 0)
    for k in range(6):
        for w in range(NV):
            column = jnp.zeros((8, 128), F32)
            for v in range(NV):
                column = jnp.where(sub == v, mix[v, k, w], column)
            mixcol[k, w] = column

    for c in range(CHUNKS):
        each(lambda s: phase1(c, s).wait_recv())
        for r in range(CHUNK // 8):
            part = pl.ds(c * CHUNK + 8 * r, 8)
            x = [recv1[j, part, :] for j in range(GROUP)]
            for bit in range(4):
                step = 8 << bit
                keep = (lane & step) == 0
                for a in range(GROUP):
                    b = a | (1 << bit)
                    if a != b:
                        low = jnp.where(keep, x[a], pltpu.roll(x[b], step, 1))
                        high = jnp.where(keep, pltpu.roll(x[a], 128 - step, 1), x[b])
                        x[a], x[b] = low, high
            for j in range(GROUP):
                send2[j, part, :] = x[j]
        each(lambda s: phase2(c, s).start())
    recv2[h] = send2[h]
    for c in range(CHUNKS):
        each(lambda s: phase2(c, s).wait_recv())

    for s in range(SOURCES):
        for side in range(2):
            for half, values in enumerate(halves(recv2[2 * s + side])):
                for r in range(ROWS // 16):
                    rtab[2 * r + half, 16 * s : 16 * s + 16, side * 128 : side * 128 + 128] = values[16 * r : 16 * r + 16]

    my_row = jnp.where(i == 0, RAD - 1, 0) * AXIAL

    def radial_copy(seg, a):
        return pltpu.make_async_remote_copy(
            src_ref=field[seg].at[:, lanes(RIM + a * RIM + my_row, AXIAL)],
            dst_ref=field[seg].at[:, lanes(EXT + a * AXIAL, AXIAL)],
            send_sem=hssem.at[seg, a],
            recv_sem=hrsem.at[seg, a],
            device_id=partner,
            device_id_type=MESH,
        )

    def behind_copy(seg):
        return pltpu.make_async_remote_copy(
            src_ref=field[seg].at[:, pl.ds(RIM, RIM)],
            dst_ref=field[seg].at[:, pl.ds(RIM + CELLS, RIM)],
            send_sem=hssem.at[seg, 4],
            recv_sem=hrsem.at[seg, 4],
            device_id=behind,
            device_id_type=MESH,
        )

    def ahead_copy(seg):
        return pltpu.make_async_remote_copy(
            src_ref=field[seg].at[:, pl.ds(CELLS, RIM)],
            dst_ref=field[seg].at[:, pl.ds(0, RIM)],
            send_sem=hssem.at[seg, 5],
            recv_sem=hrsem.at[seg, 5],
            device_id=ahead,
            device_id_type=MESH,
        )

    def send_layer(seg, j, a):
        radial_copy(seg, a).start()

        @pl.when(j == 2)
        def _():
            behind_copy(seg).start()

        @pl.when(j == 3)
        def _():
            ahead_copy(seg).start()

    def put(side, at, values):
        for half, part in enumerate(halves(jnp.concatenate(values, axis=0))):
            for r in range(ROWS // 16):
                near[side][2 * r + half, pl.ds(pl.multiple_of(at * 16, 16), 16), :] = part[16 * r : 16 * r + 16]

    def layer_of(j):
        return jnp.where(j < 2, j + 1, (j - 2) * 3)

    for copy in inputs[5:]:
        copy.wait()

    def start_layer(j, carry):
        a = layer_of(j)
        for half in range(2):
            c = 2 * a + half
            cells = lanes(c * TILE, TILE)
            first = pick(rtab[...].reshape(SOURCES * SPLIT, TILE), ohs[0, c], sids[0:1, cells], SOURCES)
            second = pick(rtab[...].reshape(SOURCES * SPLIT, TILE), ohs[1, c], sids[1:2, cells], SOURCES)
            share = jnp.broadcast_to(weight[:, cells], (8, TILE))
            begin = [share * x + (1.0 - share) * y for x, y in zip(first, second)]
            for r in range(ROWS // 8):
                field[0][8 * r : 8 * r + 8, lanes(RIM + c * TILE, TILE)] = begin[r]
            put(0, 2 + c, begin)
        send_layer(0, j, a)
        return carry

    lax.fori_loop(0, LAYERS, start_layer, 0)

    omega = freq[0]

    def rate_tile(seg, side, coef, a, half):
        c = 2 * a + half
        cells = lanes(c * TILE, TILE)
        here = lanes(RIM + c * TILE, TILE)
        own = [field[seg][8 * r : 8 * r + 8, here] for r in range(ROWS // 8)]
        mine = near[side][:, pl.ds(pl.multiple_of((2 + c) * 16, 16), 16), :].reshape(SPLIT, TILE)
        turned = jnp.dot(dmat[...], mine, preferred_element_type=F32)
        rate = [omega * (turned[8 * r : 8 * r + 8] + turned[ROWS + 8 * r : ROWS + 8 * r + 8]) for r in range(ROWS // 8)]
        table = near[side][:, pl.ds(pl.multiple_of(2 * a * 16, 16), BY_MATRIX * 16), :].reshape(BY_MATRIX * SPLIT, TILE)

        def block(start):
            return lambda r: field[seg][8 * r : 8 * r + 8, lanes(start, 128)]

        for k in range(6):
            links = nbr[k : k + 1, cells]
            sets = jnp.broadcast_to(sidn[k : k + 1, cells], (8, TILE))
            found = pick(table, ohn[k, c], sets, BY_MATRIX)
            place = links & 127
            for s in range(2 * BY_MATRIX, NEAR_BLOCKS - 1):
                start = a * RIM + s * 128
                found = from_block(block(start), place, jnp.broadcast_to(links >> 7, (8, TILE)) == 4 * a + s, found)
            found = from_block(block(EXT + a * AXIAL), place, sets == NEAR - 1, found)
            face = jnp.broadcast_to(area[k : k + 1, cells], (8, TILE))
            jump = [(found[r] - own[r]) * face for r in range(ROWS // 8)]
            for v in range(NV):
                flux = mix[v, k, 0] * jump[0]
                for w in range(1, NV):
                    flux = flux + mix[v, k, w] * jump[w]
                rate[v] = rate[v] - flux
            last = jnp.zeros((8, TILE), F32)
            for w in range(NV):
                column = mixcol[k, w]
                last = last + jnp.concatenate([column, column], axis=1) * jnp.broadcast_to(jump[NV][w : w + 1], (8, TILE))
            rate[NV] = rate[NV] - last
        step = jnp.broadcast_to(coef * dt[:, cells], (8, TILE))
        after = [field[0][8 * r : 8 * r + 8, here] - step * rate[r] for r in range(ROWS // 8)]
        for r in range(ROWS // 8):
            field[seg + 1][8 * r : 8 * r + 8, here] = after[r]
        if seg < 2:
            put(1 - side, 2 + c, after)

    def rate_layers(seg, step_at):
        side = seg % 2
        coef = SEGMENT_COEFS[seg]
        group = [layer_of(step_at * TOGETHER + n) for n in range(TOGETHER)]

        def arrived(start, at_set):
            for half in range(2):
                put(side, at_set + half, [field[seg][:, start + half * TILE : start + (half + 1) * TILE]])

        for n in range(TOGETHER):

            @pl.when(step_at * TOGETHER + n == 2)
            def _():
                ahead_copy(seg).wait_recv()
                arrived(0, 0)

            @pl.when(step_at * TOGETHER + n == 3)
            def _():
                behind_copy(seg).wait_recv()
                arrived(RIM + CELLS, 10)

        for a in group:
            radial_copy(seg, a).wait_recv()

        for a in group:
            for half in range(2):
                rate_tile(seg, side, coef, a, half)

        if seg < 2:
            for n in range(TOGETHER):
                send_layer(seg + 1, step_at * TOGETHER + n, group[n])

    for seg in range(3):

        def rate_step(step_at, carry):
            rate_layers(seg, step_at)
            return carry

        lax.fori_loop(0, LAYERS // TOGETHER, rate_step, 0)

    for v in range(NV):
        out[0:8, v, :] = field[3][8 * v : 8 * v + 8, RIM : RIM + CELLS]
    out[8] = field[3][8 * NV : 9 * NV, RIM : RIM + CELLS]

    for c in range(CHUNKS):
        each(lambda s: phase1(c, s).wait_send())
        each(lambda s: phase2(c, s).wait_send())
    for seg in range(3):
        for a in range(LAYERS):
            radial_copy(seg, a).wait_send()
        behind_copy(seg).wait_send()
        ahead_copy(seg).wait_send()


def per_device(coarse_state, send_cells, fine_source, weight, neighbours, face_area, time_step, mixing, frequency):
    vmem = pl.BlockSpec(memory_space=pltpu.VMEM)
    hbm = pl.BlockSpec(memory_space=pltpu.HBM)
    fine = pl.pallas_call(
        kernel,
        out_shape=jax.ShapeDtypeStruct((NI, NV, CELLS), F32),
        in_specs=[hbm] * 10,
        out_specs=vmem,
        scratch_shapes=[
            pltpu.VMEM((NI, NV, TILE), F32),
            pltpu.VMEM((1, CELLS), jnp.int32),
            pltpu.VMEM((2, CELLS), jnp.int32),
            pltpu.VMEM((1, CELLS), F32),
            pltpu.VMEM((6, CELLS), jnp.int32),
            pltpu.VMEM((6, CELLS), F32),
            pltpu.VMEM((1, CELLS), F32),
            pltpu.SMEM((NV, 6, NV), F32),
            pltpu.SMEM((1,), F32),
            pltpu.VMEM((SPLIT, SPLIT), BF16),
            pltpu.SemaphoreType.DMA((10,)),
            pltpu.VMEM((GROUP, ROWS, 128), F32),
            pltpu.VMEM((GROUP, ROWS, 128), F32),
            pltpu.VMEM((GROUP, ROWS, 128), F32),
            pltpu.VMEM((GROUP, ROWS, 128), F32),
            pltpu.VMEM((SPLIT // 16, SOURCES * 16, TILE), BF16),
            pltpu.VMEM((2, TILES, TILE, TILE), BF16),
            pltpu.VMEM((6, TILES, TILE, TILE), BF16),
            pltpu.VMEM((SPLIT // 16, 12 * 16, TILE), BF16),
            pltpu.VMEM((SPLIT // 16, 12 * 16, TILE), BF16),
            pltpu.VMEM((6, CELLS), jnp.int32),
            pltpu.VMEM((2, CELLS), jnp.int32),
            pltpu.VMEM((ROWS, CELLS + 3 * RIM), F32),
            pltpu.VMEM((ROWS, CELLS + 3 * RIM), F32),
            pltpu.VMEM((ROWS, CELLS + 3 * RIM), F32),
            pltpu.VMEM((ROWS, CELLS + 3 * RIM), F32),
            pltpu.VMEM((6, NV, 8, 128), F32),
            pltpu.SemaphoreType.DMA((CHUNKS, GROUP)),
            pltpu.SemaphoreType.DMA((CHUNKS, GROUP)),
            pltpu.SemaphoreType.DMA((CHUNKS, GROUP)),
            pltpu.SemaphoreType.DMA((CHUNKS, GROUP)),
            pltpu.SemaphoreType.DMA((3, 6)),
            pltpu.SemaphoreType.DMA((3, 6)),
        ],
        compiler_params=pltpu.CompilerParams(
            collective_id=0, has_side_effects=True, vmem_limit_bytes=48 * 2**20
        ),
        name="grid_sequence",
    )(
        *[
            x if x.shape == (1,) else pltpu.with_memory_space_constraint(x, pltpu.HBM)
            for x in (
                coarse_state.transpose(1, 0, 2),
                send_cells,
                fine_source,
                weight.reshape(1, CELLS),
                neighbours,
                face_area,
                time_step.reshape(1, CELLS),
                mixing.transpose(1, 0, 2),
                frequency,
                jnp.asarray(spectral_rows()),
            )
        ]
    )
    return fine.transpose(1, 0, 2)


def solution(mesh):
    placed = (
        P(None, None, ("theta", "inst")),
        P(("theta", "inst"), None),
        P(None, ("theta", "inst")),
        P(("theta", "inst")),
        P(None, ("theta", "inst")),
        P(None, ("theta", "inst")),
        P(("theta", "inst")),
        P(),
        P(),
    )
    return jax.shard_map(
        per_device,
        mesh=mesh,
        in_specs=placed,
        out_specs=P(None, None, ("theta", "inst")),
        check_vma=False,
    )
```

```python
import functools

import jax
import jax.numpy as jnp
import numpy as np
from jax import lax
from jax.experimental import pallas as pl
from jax.experimental.pallas import tpu as pltpu
from jax.sharding import PartitionSpec as P

NV = 5
NI = 9
AXIAL = 128
RAD = 4
LAYERS = 4
RIM = 512
CELLS = 2048
EXT = CELLS + 2 * RIM
ROWS = 48
SPLIT = 2 * ROWS
TILE = 256
TILES = CELLS // TILE
NEAR = 7
NEAR_BLOCKS = 13
BY_MATRIX = 5
GROUP = 16
CHUNK = 24
CHUNKS = ROWS // CHUNK
SOURCES = 8

SEGMENT_COEFS = (0.6, 0.6, 1.0)
MESH = pl.DeviceIdType.MESH
F32 = jnp.float32
BF16 = jnp.bfloat16


def spectral_rows():
    offsets = np.arange(NI)[:, None] - np.arange(NI)[None, :]
    sine = np.where(offsets == 0, 1.0, np.sin(np.pi * offsets / NI))
    matrix = np.where(offsets == 0, 0.0, 0.5 * np.where(offsets % 2 == 0, 1.0, -1.0) / sine)
    place = np.array([[v * 8 + n if n < 8 else NV * 8 + v for n in range(NI)] for v in range(NV)])
    full = np.zeros((ROWS, ROWS), np.float32)
    for v in range(NV):
        full[np.ix_(place[v], place[v])] = matrix
    high = full.astype(BF16)
    low = (full - high.astype(np.float32)).astype(BF16)
    twice = [np.concatenate([x[:, r : r + 16]] * 2, 1) for x in (high, low) for r in range(0, ROWS, 16)]
    return np.concatenate([np.concatenate(twice[:3], 1), np.concatenate(twice[3:], 1)], 0)


def halves(x):
    high = x.astype(BF16)
    return high, (x - high.astype(F32)).astype(BF16)


def one_hot(low):
    hit = lax.broadcasted_iota(jnp.int32, (TILE, TILE), 0) == low
    return jnp.where(hit, 1.0, 0.0).astype(BF16)


def pick(table, hot, sets, count):
    found = jnp.dot(table, hot, preferred_element_type=F32)
    sets = jnp.broadcast_to(sets, (8, TILE))
    masks = [sets == s for s in range(1, count)]
    rows = []
    for r in range(0, ROWS, 8):
        parts = []
        for half in range(2):
            base = ((r // 16) * 2 + half) * count * 16 + r % 16
            value = found[base : base + 8]
            for s in range(1, count):
                value = jnp.where(masks[s - 1], found[base + s * 16 : base + s * 16 + 8], value)
            parts.append(value)
        rows.append(parts[0] + parts[1])
    return rows


def from_block(block, place, masks, values):
    merged = []
    for r in range(ROWS // 8):
        rows = block(r)
        found = [
            jnp.take_along_axis(rows, jnp.broadcast_to(place[:, at : at + 128], (8, 128)), axis=1, mode="promise_in_bounds")
            for at in range(0, TILE, 128)
        ]
        merged.append(jnp.where(masks, jnp.concatenate(found, axis=1), values[r]))
    return merged


def kernel(
    coarse_in, send_in, fsrc_in, weight_in, nbr_in, area_in, dt_in, mix_in, freq_in, dmat_in, out,
    coarse, send, fsrc, weight, nbr, area, dt, mix, freq, dmat, isem, outg, recv1, send2, recv2, rtab, ohs, ohn, near0, near1, sidn, sids, field0, field1, field2, mixcol,
    ssem1, rsem1, ssem2, rsem2, hssem, hrsem,
):
    inputs = [
        pltpu.make_async_copy(src, dst, isem.at[at])
        for at, (src, dst) in enumerate(
            [
                (coarse_in, coarse), (send_in, send), (fsrc_in, fsrc), (nbr_in, nbr), (mix_in, mix),
                (freq_in, freq), (weight_in, weight), (area_in, area), (dt_in, dt), (dmat_in, dmat),
            ]
        )
    ]
    for copy in inputs:
        copy.start()

    field = [field0, field1, field2]
    near = [near0, near1]
    t = lax.axis_index("theta")
    i = lax.axis_index("inst")
    count = 128
    z, x_lo, y, core = t // 16, t // 8 % 2, t // 2 % 4, t % 2
    g = z * 2 + core
    h = y * 4 + x_lo * 2 + i

    def in_phase1(s):
        other = (g + s) % GROUP
        return ((other // 2 * 2 + x_lo) * 4 + y) * 2 + other % 2, i

    def in_phase2(s):
        other = (h + s) % GROUP
        return ((z * 2 + other // 2 % 2) * 4 + other // 4) * 2 + core, other % 2

    ahead = ((t + 1) % count, i)
    behind = ((t + count - 1) % count, i)
    partner = (t, 1 - i)

    def lanes(start, size):
        return pl.ds(pl.multiple_of(start, 128), size)

    for arriving in (recv1, recv2):
        arriving[:, ROWS - 8 :, :] = jnp.zeros((GROUP, 8, 128), F32)
    barrier = pltpu.get_barrier_semaphore()

    def greet(s, carry):
        pl.semaphore_signal(barrier, inc=1, device_id=in_phase1(s), device_id_type=MESH)
        pl.semaphore_signal(barrier, inc=1, device_id=in_phase2(s), device_id_type=MESH)
        return carry

    lax.fori_loop(1, GROUP, greet, 0)
    pl.semaphore_signal(barrier, inc=1, device_id=ahead, device_id_type=MESH)
    pl.semaphore_signal(barrier, inc=1, device_id=behind, device_id_type=MESH)

    inputs[0].wait()
    inputs[1].wait()

    rows = jnp.concatenate(
        [coarse[0:8, v, :] for v in range(NV)] + [coarse[8], jnp.zeros((ROWS - NV * NI, TILE), F32)], axis=0
    )
    table = jnp.concatenate(halves(rows), axis=0)

    lane = lax.broadcasted_iota(jnp.int32, (8, 128), 1)

    for c in range(TILES):
        even = send[:, lanes(c * TILE, 128)]
        odd = send[:, lanes(c * TILE + 128, 128)]
        keep = (lane[:1] & 16) == 0
        first = jnp.where(keep, even, pltpu.roll(odd, 16, 1))
        second = jnp.where(keep, pltpu.roll(even, 112, 1), odd)
        low = jnp.maximum(jnp.concatenate([first, second], axis=1), 0)
        found = jnp.dot(table, one_hot(low), preferred_element_type=F32)
        found = found[:ROWS] + found[ROWS:]
        outg[2 * c] = found[:, :128]
        outg[2 * c + 1] = found[:, 128:]

    pl.semaphore_wait(barrier, 2 * (GROUP - 1) + 2)

    def phase1(c, s):
        part = pl.ds(c * CHUNK, min(CHUNK, NV * NI - c * CHUNK))
        return pltpu.make_async_remote_copy(
            src_ref=outg.at[(g + s) % GROUP, part],
            dst_ref=recv1.at[g, part],
            send_sem=ssem1.at[c, s],
            recv_sem=rsem1.at[c, s],
            device_id=in_phase1(s),
            device_id_type=MESH,
        )

    def phase2(c, s):
        part = pl.ds(c * CHUNK, min(CHUNK, NV * NI - c * CHUNK))
        return pltpu.make_async_remote_copy(
            src_ref=send2.at[(h + s) % GROUP, part],
            dst_ref=recv2.at[h, part],
            send_sem=ssem2.at[c, s],
            recv_sem=rsem2.at[c, s],
            device_id=in_phase2(s),
            device_id_type=MESH,
        )

    def each(action):
        for s in range(1, GROUP):
            action(s)

    for c in range(CHUNKS):
        each(lambda s: phase1(c, s).start())
    recv1[g] = outg[g]

    for copy in inputs[2:5]:
        copy.wait()

    slots = fsrc[...]
    owner = slots >> 3
    from_g = (owner >> 5) * 2 + ((owner >> 1) & 1)
    from_h = ((owner >> 2) & 3) * 4 + ((owner >> 4) & 1) * 2 + (owner & 1)
    places = from_h * 128 + from_g * 8 + (slots & 7)
    low_places = places & 255
    sids[...] = places >> 8
    fsrc[...] = low_places
    links = nbr[...]
    layer = lax.broadcasted_iota(jnp.int32, (6, CELLS), 1) >> 9
    sidn[...] = jnp.where(links >= EXT, NEAR - 1, (links >> 8) - 2 * layer)

    def hot_start(c, carry):
        cells = pl.ds(pl.multiple_of(c * TILE, TILE), TILE)
        for side in range(2):
            ohs[side, c] = one_hot(fsrc[side : side + 1, cells])
        for k in range(6):
            ohn[k, c] = one_hot(nbr[k : k + 1, cells] & 255)
        return carry

    lax.fori_loop(0, TILES, hot_start, 0)
    sub = lax.broadcasted_iota(jnp.int32, (8, 128), 0)
    for k in range(6):
        for w in range(NV):
            column = jnp.zeros((8, 128), F32)
            for v in range(NV):
                column = jnp.where(sub == v, mix[v, k, w], column)
            mixcol[k, w] = column

    for c in range(CHUNKS):
        each(lambda s: phase1(c, s).wait_recv())
        for r in range(CHUNK // 8):
            part = pl.ds(c * CHUNK + 8 * r, 8)
            x = [recv1[j, part, :] for j in range(GROUP)]
            for bit in range(4):
                step = 8 << bit
                keep = (lane & step) == 0
                for a in range(GROUP):
                    b = a | (1 << bit)
                    if a != b:
                        low = jnp.where(keep, x[a], pltpu.roll(x[b], step, 1))
                        high = jnp.where(keep, pltpu.roll(x[a], 128 - step, 1), x[b])
                        x[a], x[b] = low, high
            for j in range(GROUP):
                send2[j, part, :] = x[j]
        each(lambda s: phase2(c, s).start())
    recv2[h] = send2[h]
    for c in range(CHUNKS):
        each(lambda s: phase2(c, s).wait_recv())

    for s in range(SOURCES):
        for side in range(2):
            for half, values in enumerate(halves(recv2[2 * s + side])):
                for r in range(ROWS // 16):
                    rtab[2 * r + half, 16 * s : 16 * s + 16, side * 128 : side * 128 + 128] = values[16 * r : 16 * r + 16]

    my_row = jnp.where(i == 0, RAD - 1, 0) * AXIAL

    def radial_copy(seg, a):
        return pltpu.make_async_remote_copy(
            src_ref=field[seg].at[:, lanes(RIM + a * RIM + my_row, AXIAL)],
            dst_ref=field[seg].at[:, lanes(EXT + a * AXIAL, AXIAL)],
            send_sem=hssem.at[seg, a],
            recv_sem=hrsem.at[seg, a],
            device_id=partner,
            device_id_type=MESH,
        )

    def behind_copy(seg):
        return pltpu.make_async_remote_copy(
            src_ref=field[seg].at[:, pl.ds(RIM, RIM)],
            dst_ref=field[seg].at[:, pl.ds(RIM + CELLS, RIM)],
            send_sem=hssem.at[seg, 4],
            recv_sem=hrsem.at[seg, 4],
            device_id=behind,
            device_id_type=MESH,
        )

    def ahead_copy(seg):
        return pltpu.make_async_remote_copy(
            src_ref=field[seg].at[:, pl.ds(CELLS, RIM)],
            dst_ref=field[seg].at[:, pl.ds(0, RIM)],
            send_sem=hssem.at[seg, 5],
            recv_sem=hrsem.at[seg, 5],
            device_id=ahead,
            device_id_type=MESH,
        )

    def send_layer(seg, a):
        radial_copy(seg, a).start()

        @pl.when(a == 0)
        def _():
            behind_copy(seg).start()

        @pl.when(a == LAYERS - 1)
        def _():
            ahead_copy(seg).start()

    def put(side, at, values):
        for half, part in enumerate(halves(jnp.concatenate(values, axis=0))):
            for r in range(ROWS // 16):
                near[side][2 * r + half, pl.ds(pl.multiple_of(at * 16, 16), 16), :] = part[16 * r : 16 * r + 16]

    def layer_of(seg, j):
        outer = (j - 2) * 3 if seg % 2 == 0 else (3 - j) * 3
        return jnp.where(j < 2, j + 1, outer)

    for copy in inputs[5:]:
        copy.wait()

    def start_layer(j, carry):
        a = layer_of(1, j)
        for half in range(2):
            c = 2 * a + half
            cells = lanes(c * TILE, TILE)
            first = pick(rtab[...].reshape(SOURCES * SPLIT, TILE), ohs[0, c], sids[0:1, cells], SOURCES)
            second = pick(rtab[...].reshape(SOURCES * SPLIT, TILE), ohs[1, c], sids[1:2, cells], SOURCES)
            share = jnp.broadcast_to(weight[:, cells], (8, TILE))
            begin = [share * x + (1.0 - share) * y for x, y in zip(first, second)]
            for r in range(ROWS // 8):
                field[0][8 * r : 8 * r + 8, lanes(RIM + c * TILE, TILE)] = begin[r]
            put(0, 2 + c, begin)
        send_layer(0, a)
        return carry

    lax.fori_loop(0, LAYERS, start_layer, 0)

    omega = freq[0]

    def rate_tile(seg, side, coef, a, half):
        c = 2 * a + half
        cells = lanes(c * TILE, TILE)
        here = lanes(RIM + c * TILE, TILE)
        own = [field[seg][8 * r : 8 * r + 8, here] for r in range(ROWS // 8)]
        mine = near[side][:, pl.ds(pl.multiple_of((2 + c) * 16, 16), 16), :].reshape(SPLIT, TILE)
        turned = jnp.dot(dmat[...], mine, preferred_element_type=F32)
        rate = [omega * (turned[8 * r : 8 * r + 8] + turned[ROWS + 8 * r : ROWS + 8 * r + 8]) for r in range(ROWS // 8)]
        table = near[side][:, pl.ds(pl.multiple_of(2 * a * 16, 16), BY_MATRIX * 16), :].reshape(BY_MATRIX * SPLIT, TILE)

        def block(start):
            return lambda r: field[seg][8 * r : 8 * r + 8, lanes(start, 128)]

        for k in range(6):
            links = nbr[k : k + 1, cells]
            sets = jnp.broadcast_to(sidn[k : k + 1, cells], (8, TILE))
            found = pick(table, ohn[k, c], sets, BY_MATRIX)
            place = links & 127
            for s in range(2 * BY_MATRIX, NEAR_BLOCKS - 1):
                start = a * RIM + s * 128
                found = from_block(block(start), place, jnp.broadcast_to(links >> 7, (8, TILE)) == 4 * a + s, found)
            found = from_block(block(EXT + a * AXIAL), place, sets == NEAR - 1, found)
            face = jnp.broadcast_to(area[k : k + 1, cells], (8, TILE))
            jump = [(found[r] - own[r]) * face for r in range(ROWS // 8)]
            for v in range(NV):
                flux = mix[v, k, 0] * jump[0]
                for w in range(1, NV):
                    flux = flux + mix[v, k, w] * jump[w]
                rate[v] = rate[v] - flux
            last = jnp.zeros((8, TILE), F32)
            for w in range(NV):
                column = mixcol[k, w]
                last = last + jnp.concatenate([column, column], axis=1) * jnp.broadcast_to(jump[NV][w : w + 1], (8, TILE))
            rate[NV] = rate[NV] - last
        step = jnp.broadcast_to(coef * dt[:, cells], (8, TILE))
        after = [field[0][8 * r : 8 * r + 8, here] - step * rate[r] for r in range(ROWS // 8)]
        if seg < 2:
            for r in range(ROWS // 8):
                field[seg + 1][8 * r : 8 * r + 8, here] = after[r]
            put(1 - side, 2 + c, after)
        else:
            for v in range(NV):
                out[0:8, v, cells] = after[v]
            out[8, :, cells] = after[NV][:NV]

    def rate_layer(seg, j):
        side = seg % 2
        a = layer_of(seg, j)

        def arrived(start, at_set):
            for half in range(2):
                put(side, at_set + half, [field[seg][:, start + half * TILE : start + (half + 1) * TILE]])

        @pl.when(a == 0)
        def _():
            ahead_copy(seg).wait_recv()
            arrived(0, 0)

        @pl.when(a == LAYERS - 1)
        def _():
            behind_copy(seg).wait_recv()
            arrived(RIM + CELLS, 10)

        radial_copy(seg, a).wait_recv()
        for half in range(2):
            rate_tile(seg, side, SEGMENT_COEFS[seg], a, half)
        if seg < 2:
            send_layer(seg + 1, a)

    for seg in range(3):

        def rate_step(j, carry):
            rate_layer(seg, j)
            return carry

        lax.fori_loop(0, LAYERS, rate_step, 0)

    for c in range(CHUNKS):
        each(lambda s: phase1(c, s).wait_send())
        each(lambda s: phase2(c, s).wait_send())
    for seg in range(3):
        for a in range(LAYERS):
            radial_copy(seg, a).wait_send()
        behind_copy(seg).wait_send()
        ahead_copy(seg).wait_send()


def per_device(coarse_state, send_cells, fine_source, weight, neighbours, face_area, time_step, mixing, frequency):
    vmem = pl.BlockSpec(memory_space=pltpu.VMEM)
    hbm = pl.BlockSpec(memory_space=pltpu.HBM)
    fine = pl.pallas_call(
        kernel,
        out_shape=jax.ShapeDtypeStruct((NI, NV, CELLS), F32),
        in_specs=[hbm] * 10,
        out_specs=vmem,
        scratch_shapes=[
            pltpu.VMEM((NI, NV, TILE), F32),
            pltpu.VMEM((1, CELLS), jnp.int32),
            pltpu.VMEM((2, CELLS), jnp.int32),
            pltpu.VMEM((1, CELLS), F32),
            pltpu.VMEM((6, CELLS), jnp.int32),
            pltpu.VMEM((6, CELLS), F32),
            pltpu.VMEM((1, CELLS), F32),
            pltpu.SMEM((NV, 6, NV), F32),
            pltpu.SMEM((1,), F32),
            pltpu.VMEM((SPLIT, SPLIT), BF16),
            pltpu.SemaphoreType.DMA((10,)),
            pltpu.VMEM((GROUP, ROWS, 128), F32),
            pltpu.VMEM((GROUP, ROWS, 128), F32),
            pltpu.VMEM((GROUP, ROWS, 128), F32),
            pltpu.VMEM((GROUP, ROWS, 128), F32),
            pltpu.VMEM((SPLIT // 16, SOURCES * 16, TILE), BF16),
            pltpu.VMEM((2, TILES, TILE, TILE), BF16),
            pltpu.VMEM((6, TILES, TILE, TILE), BF16),
            pltpu.VMEM((SPLIT // 16, 12 * 16, TILE), BF16),
            pltpu.VMEM((SPLIT // 16, 12 * 16, TILE), BF16),
            pltpu.VMEM((6, CELLS), jnp.int32),
            pltpu.VMEM((2, CELLS), jnp.int32),
            pltpu.VMEM((ROWS, CELLS + 3 * RIM), F32),
            pltpu.VMEM((ROWS, CELLS + 3 * RIM), F32),
            pltpu.VMEM((ROWS, CELLS + 3 * RIM), F32),
            pltpu.VMEM((6, NV, 8, 128), F32),
            pltpu.SemaphoreType.DMA((CHUNKS, GROUP)),
            pltpu.SemaphoreType.DMA((CHUNKS, GROUP)),
            pltpu.SemaphoreType.DMA((CHUNKS, GROUP)),
            pltpu.SemaphoreType.DMA((CHUNKS, GROUP)),
            pltpu.SemaphoreType.DMA((3, 6)),
            pltpu.SemaphoreType.DMA((3, 6)),
        ],
        compiler_params=pltpu.CompilerParams(
            collective_id=0, has_side_effects=True, vmem_limit_bytes=48 * 2**20
        ),
        name="grid_sequence",
    )(
        *[
            x if x.shape == (1,) else pltpu.with_memory_space_constraint(x, pltpu.HBM)
            for x in (
                coarse_state.transpose(1, 0, 2),
                send_cells,
                fine_source,
                weight.reshape(1, CELLS),
                neighbours,
                face_area,
                time_step.reshape(1, CELLS),
                mixing.transpose(1, 0, 2),
                frequency,
                jnp.asarray(spectral_rows()),
            )
        ]
    )
    return fine.transpose(1, 0, 2)


def solution(mesh):
    placed = (
        P(None, None, ("theta", "inst")),
        P(("theta", "inst"), None),
        P(None, ("theta", "inst")),
        P(("theta", "inst")),
        P(None, ("theta", "inst")),
        P(None, ("theta", "inst")),
        P(("theta", "inst")),
        P(),
        P(),
    )
    return jax.shard_map(
        per_device,
        mesh=mesh,
        in_specs=placed,
        out_specs=P(None, None, ("theta", "inst")),
        check_vma=False,
    )
```

```python
import functools

import jax
import jax.numpy as jnp
import numpy as np
from jax import lax
from jax.experimental import pallas as pl
from jax.experimental.pallas import tpu as pltpu
from jax.sharding import PartitionSpec as P

NV = 5
NI = 9
AXIAL = 128
RAD = 4
LAYERS = 4
RIM = 512
CELLS = 2048
EXT = CELLS + 2 * RIM
ROWS = 48
SPLIT = 2 * ROWS
TILE = 256
TILES = CELLS // TILE
NEAR = 7
NEAR_BLOCKS = 13
BY_MATRIX = 5
GROUP = 16
CHUNK = 24
CHUNKS = ROWS // CHUNK
FIRST = (8, 7, 9, 6, 10, 5, 11, 4, 12, 3, 13, 2, 14, 1, 15)
SOURCES = 8

SEGMENT_COEFS = (0.6, 0.6, 1.0)
MESH = pl.DeviceIdType.MESH
F32 = jnp.float32
BF16 = jnp.bfloat16


def spectral_rows():
    offsets = np.arange(NI)[:, None] - np.arange(NI)[None, :]
    sine = np.where(offsets == 0, 1.0, np.sin(np.pi * offsets / NI))
    matrix = np.where(offsets == 0, 0.0, 0.5 * np.where(offsets % 2 == 0, 1.0, -1.0) / sine)
    place = np.array([[v * 8 + n if n < 8 else NV * 8 + v for n in range(NI)] for v in range(NV)])
    full = np.zeros((ROWS, ROWS), np.float32)
    for v in range(NV):
        full[np.ix_(place[v], place[v])] = matrix
    high = full.astype(BF16)
    low = (full - high.astype(np.float32)).astype(BF16)
    twice = [np.concatenate([x[:, r : r + 16]] * 2, 1) for x in (high, low) for r in range(0, ROWS, 16)]
    return np.concatenate([np.concatenate(twice[:3], 1), np.concatenate(twice[3:], 1)], 0)


def halves(x):
    high = x.astype(BF16)
    return high, (x - high.astype(F32)).astype(BF16)


def one_hot(low):
    hit = lax.broadcasted_iota(jnp.int32, (TILE, TILE), 0) == low
    return jnp.where(hit, 1.0, 0.0).astype(BF16)


def pick(table, hot, sets, count):
    found = jnp.dot(table, hot, preferred_element_type=F32)
    sets = jnp.broadcast_to(sets, (8, TILE))
    masks = [sets == s for s in range(1, count)]
    rows = []
    for r in range(0, ROWS, 8):
        parts = []
        for half in range(2):
            base = ((r // 16) * 2 + half) * count * 16 + r % 16
            value = found[base : base + 8]
            for s in range(1, count):
                value = jnp.where(masks[s - 1], found[base + s * 16 : base + s * 16 + 8], value)
            parts.append(value)
        rows.append(parts[0] + parts[1])
    return rows


def from_block(block, place, masks, values):
    merged = []
    for r in range(ROWS // 8):
        rows = block(r)
        found = [
            jnp.take_along_axis(rows, jnp.broadcast_to(place[:, at : at + 128], (8, 128)), axis=1, mode="promise_in_bounds")
            for at in range(0, TILE, 128)
        ]
        merged.append(jnp.where(masks, jnp.concatenate(found, axis=1), values[r]))
    return merged


def kernel(
    coarse_in, send_in, fsrc_in, weight_in, nbr_in, area_in, dt_in, mix_in, freq_in, dmat_in, out,
    coarse, send, fsrc, weight, nbr, area, dt, mix, freq, dmat, isem, outg, recv1, send2, recv2, rtab, ohs, ohn, near0, near1, sidn, sids, field0, field1, field2, mixcol,
    ssem1, rsem1, ssem2, rsem2, hssem, hrsem,
):
    inputs = [
        pltpu.make_async_copy(src, dst, isem.at[at])
        for at, (src, dst) in enumerate(
            [
                (coarse_in, coarse), (send_in, send), (fsrc_in, fsrc), (nbr_in, nbr), (mix_in, mix),
                (freq_in, freq), (weight_in, weight), (area_in, area), (dt_in, dt), (dmat_in, dmat),
            ]
        )
    ]
    for copy in inputs:
        copy.start()

    field = [field0, field1, field2]
    near = [near0, near1]
    t = lax.axis_index("theta")
    i = lax.axis_index("inst")
    count = 128
    z, x_lo, y, core = t // 16, t // 8 % 2, t // 2 % 4, t % 2
    g = z * 2 + core
    h = y * 4 + x_lo * 2 + i

    def in_phase1(s):
        other = (g + s) % GROUP
        return ((other // 2 * 2 + x_lo) * 4 + y) * 2 + other % 2, i

    def in_phase2(s):
        other = (h + s) % GROUP
        return ((z * 2 + other // 2 % 2) * 4 + other // 4) * 2 + core, other % 2

    ahead = ((t + 1) % count, i)
    behind = ((t + count - 1) % count, i)
    partner = (t, 1 - i)

    def lanes(start, size):
        return pl.ds(pl.multiple_of(start, 128), size)

    for arriving in (recv1, recv2):
        arriving[:, ROWS - 8 :, :] = jnp.zeros((GROUP, 8, 128), F32)
    barrier = pltpu.get_barrier_semaphore()

    def greet(s, carry):
        pl.semaphore_signal(barrier, inc=1, device_id=in_phase1(s), device_id_type=MESH)
        pl.semaphore_signal(barrier, inc=1, device_id=in_phase2(s), device_id_type=MESH)
        return carry

    lax.fori_loop(1, GROUP, greet, 0)
    pl.semaphore_signal(barrier, inc=1, device_id=ahead, device_id_type=MESH)
    pl.semaphore_signal(barrier, inc=1, device_id=behind, device_id_type=MESH)

    inputs[0].wait()
    inputs[1].wait()

    rows = jnp.concatenate(
        [coarse[0:8, v, :] for v in range(NV)] + [coarse[8], jnp.zeros((ROWS - NV * NI, TILE), F32)], axis=0
    )
    table = jnp.concatenate(halves(rows), axis=0)

    lane = lax.broadcasted_iota(jnp.int32, (8, 128), 1)

    for c in range(TILES):
        even = send[:, lanes(c * TILE, 128)]
        odd = send[:, lanes(c * TILE + 128, 128)]
        keep = (lane[:1] & 16) == 0
        first = jnp.where(keep, even, pltpu.roll(odd, 16, 1))
        second = jnp.where(keep, pltpu.roll(even, 112, 1), odd)
        low = jnp.maximum(jnp.concatenate([first, second], axis=1), 0)
        found = jnp.dot(table, one_hot(low), preferred_element_type=F32)
        found = found[:ROWS] + found[ROWS:]
        outg[2 * c] = found[:, :128]
        outg[2 * c + 1] = found[:, 128:]

    pl.semaphore_wait(barrier, 2 * (GROUP - 1) + 2)

    def phase1(c, s):
        part = pl.ds(c * CHUNK, min(CHUNK, NV * NI - c * CHUNK))
        return pltpu.make_async_remote_copy(
            src_ref=outg.at[(g + s) % GROUP, part],
            dst_ref=recv1.at[g, part],
            send_sem=ssem1.at[c, s],
            recv_sem=rsem1.at[c, s],
            device_id=in_phase1(s),
            device_id_type=MESH,
        )

    def phase2(c, s):
        part = pl.ds(c * CHUNK, min(CHUNK, NV * NI - c * CHUNK))
        return pltpu.make_async_remote_copy(
            src_ref=send2.at[(h + s) % GROUP, part],
            dst_ref=recv2.at[h, part],
            send_sem=ssem2.at[c, s],
            recv_sem=rsem2.at[c, s],
            device_id=in_phase2(s),
            device_id_type=MESH,
        )

    def each(action):
        for s in range(1, GROUP):
            action(s)

    for c in range(CHUNKS):
        for s in FIRST:
            phase1(c, s).start()
    recv1[g] = outg[g]

    for copy in inputs[2:5]:
        copy.wait()

    slots = fsrc[...]
    owner = slots >> 3
    from_g = (owner >> 5) * 2 + ((owner >> 1) & 1)
    from_h = ((owner >> 2) & 3) * 4 + ((owner >> 4) & 1) * 2 + (owner & 1)
    places = from_h * 128 + from_g * 8 + (slots & 7)
    low_places = places & 255
    sids[...] = places >> 8
    fsrc[...] = low_places
    links = nbr[...]
    layer = lax.broadcasted_iota(jnp.int32, (6, CELLS), 1) >> 9
    sidn[...] = jnp.where(links >= EXT, NEAR - 1, (links >> 8) - 2 * layer)

    def hot_start(c, carry):
        cells = pl.ds(pl.multiple_of(c * TILE, TILE), TILE)
        for side in range(2):
            ohs[side, c] = one_hot(fsrc[side : side + 1, cells])
        for k in range(6):
            ohn[k, c] = one_hot(nbr[k : k + 1, cells] & 255)
        return carry

    lax.fori_loop(0, TILES, hot_start, 0)
    sub = lax.broadcasted_iota(jnp.int32, (8, 128), 0)
    for k in range(6):
        for w in range(NV):
            column = jnp.zeros((8, 128), F32)
            for v in range(NV):
                column = jnp.where(sub == v, mix[v, k, w], column)
            mixcol[k, w] = column

    for c in range(CHUNKS):
        each(lambda s: phase1(c, s).wait_recv())
        for r in range(CHUNK // 8):
            part = pl.ds(c * CHUNK + 8 * r, 8)
            x = [recv1[j, part, :] for j in range(GROUP)]
            for bit in range(4):
                step = 8 << bit
                keep = (lane & step) == 0
                for a in range(GROUP):
                    b = a | (1 << bit)
                    if a != b:
                        low = jnp.where(keep, x[a], pltpu.roll(x[b], step, 1))
                        high = jnp.where(keep, pltpu.roll(x[a], 128 - step, 1), x[b])
                        x[a], x[b] = low, high
            for j in range(GROUP):
                send2[j, part, :] = x[j]
        each(lambda s: phase2(c, s).start())
    recv2[h] = send2[h]
    for c in range(CHUNKS):
        each(lambda s: phase2(c, s).wait_recv())

    for s in range(SOURCES):
        for side in range(2):
            for half, values in enumerate(halves(recv2[2 * s + side])):
                for r in range(ROWS // 16):
                    rtab[2 * r + half, 16 * s : 16 * s + 16, side * 128 : side * 128 + 128] = values[16 * r : 16 * r + 16]

    my_row = jnp.where(i == 0, RAD - 1, 0) * AXIAL

    def radial_copy(seg, a):
        return pltpu.make_async_remote_copy(
            src_ref=field[seg].at[:, lanes(RIM + a * RIM + my_row, AXIAL)],
            dst_ref=field[seg].at[:, lanes(EXT + a * AXIAL, AXIAL)],
            send_sem=hssem.at[seg, a],
            recv_sem=hrsem.at[seg, a],
            device_id=partner,
            device_id_type=MESH,
        )

    def behind_copy(seg):
        return pltpu.make_async_remote_copy(
            src_ref=field[seg].at[:, pl.ds(RIM, RIM)],
            dst_ref=field[seg].at[:, pl.ds(RIM + CELLS, RIM)],
            send_sem=hssem.at[seg, 4],
            recv_sem=hrsem.at[seg, 4],
            device_id=behind,
            device_id_type=MESH,
        )

    def ahead_copy(seg):
        return pltpu.make_async_remote_copy(
            src_ref=field[seg].at[:, pl.ds(CELLS, RIM)],
            dst_ref=field[seg].at[:, pl.ds(0, RIM)],
            send_sem=hssem.at[seg, 5],
            recv_sem=hrsem.at[seg, 5],
            device_id=ahead,
            device_id_type=MESH,
        )

    def send_layer(seg, a):
        radial_copy(seg, a).start()

        @pl.when(a == 0)
        def _():
            behind_copy(seg).start()

        @pl.when(a == LAYERS - 1)
        def _():
            ahead_copy(seg).start()

    def put(side, at, values):
        for half, part in enumerate(halves(jnp.concatenate(values, axis=0))):
            for r in range(ROWS // 16):
                near[side][2 * r + half, pl.ds(pl.multiple_of(at * 16, 16), 16), :] = part[16 * r : 16 * r + 16]

    def layer_of(seg, j):
        outer = (j - 2) * 3 if seg % 2 == 0 else (3 - j) * 3
        return jnp.where(j < 2, j + 1, outer)

    for copy in inputs[5:]:
        copy.wait()

    def start_layer(j, carry):
        a = layer_of(1, j)
        for half in range(2):
            c = 2 * a + half
            cells = lanes(c * TILE, TILE)
            first = pick(rtab[...].reshape(SOURCES * SPLIT, TILE), ohs[0, c], sids[0:1, cells], SOURCES)
            second = pick(rtab[...].reshape(SOURCES * SPLIT, TILE), ohs[1, c], sids[1:2, cells], SOURCES)
            share = jnp.broadcast_to(weight[:, cells], (8, TILE))
            begin = [share * x + (1.0 - share) * y for x, y in zip(first, second)]
            for r in range(ROWS // 8):
                field[0][8 * r : 8 * r + 8, lanes(RIM + c * TILE, TILE)] = begin[r]
            put(0, 2 + c, begin)
        send_layer(0, a)
        return carry

    lax.fori_loop(0, LAYERS, start_layer, 0)

    omega = freq[0]

    def rate_tile(seg, side, coef, a, half):
        c = 2 * a + half
        cells = lanes(c * TILE, TILE)
        here = lanes(RIM + c * TILE, TILE)
        own = [field[seg][8 * r : 8 * r + 8, here] for r in range(ROWS // 8)]
        mine = near[side][:, pl.ds(pl.multiple_of((2 + c) * 16, 16), 16), :].reshape(SPLIT, TILE)
        turned = jnp.dot(dmat[...], mine, preferred_element_type=F32)
        rate = [omega * (turned[8 * r : 8 * r + 8] + turned[ROWS + 8 * r : ROWS + 8 * r + 8]) for r in range(ROWS // 8)]
        table = near[side][:, pl.ds(pl.multiple_of(2 * a * 16, 16), BY_MATRIX * 16), :].reshape(BY_MATRIX * SPLIT, TILE)

        def block(start):
            return lambda r: field[seg][8 * r : 8 * r + 8, lanes(start, 128)]

        for k in range(6):
            links = nbr[k : k + 1, cells]
            sets = jnp.broadcast_to(sidn[k : k + 1, cells], (8, TILE))
            found = pick(table, ohn[k, c], sets, BY_MATRIX)
            place = links & 127
            for s in range(2 * BY_MATRIX, NEAR_BLOCKS - 1):
                start = a * RIM + s * 128
                found = from_block(block(start), place, jnp.broadcast_to(links >> 7, (8, TILE)) == 4 * a + s, found)
            found = from_block(block(EXT + a * AXIAL), place, sets == NEAR - 1, found)
            face = jnp.broadcast_to(area[k : k + 1, cells], (8, TILE))
            jump = [(found[r] - own[r]) * face for r in range(ROWS // 8)]
            for v in range(NV):
                flux = mix[v, k, 0] * jump[0]
                for w in range(1, NV):
                    flux = flux + mix[v, k, w] * jump[w]
                rate[v] = rate[v] - flux
            last = jnp.zeros((8, TILE), F32)
            for w in range(NV):
                column = mixcol[k, w]
                last = last + jnp.concatenate([column, column], axis=1) * jnp.broadcast_to(jump[NV][w : w + 1], (8, TILE))
            rate[NV] = rate[NV] - last
        step = jnp.broadcast_to(coef * dt[:, cells], (8, TILE))
        after = [field[0][8 * r : 8 * r + 8, here] - step * rate[r] for r in range(ROWS // 8)]
        if seg < 2:
            for r in range(ROWS // 8):
                field[seg + 1][8 * r : 8 * r + 8, here] = after[r]
            put(1 - side, 2 + c, after)
        else:
            for v in range(NV):
                out[0:8, v, cells] = after[v]
            out[8, :, cells] = after[NV][:NV]

    def rate_layer(seg, j):
        side = seg % 2
        a = layer_of(seg, j)

        def arrived(start, at_set):
            for half in range(2):
                put(side, at_set + half, [field[seg][:, start + half * TILE : start + (half + 1) * TILE]])

        @pl.when(a == 0)
        def _():
            ahead_copy(seg).wait_recv()
            arrived(0, 0)

        @pl.when(a == LAYERS - 1)
        def _():
            behind_copy(seg).wait_recv()
            arrived(RIM + CELLS, 10)

        radial_copy(seg, a).wait_recv()
        for half in range(2):
            rate_tile(seg, side, SEGMENT_COEFS[seg], a, half)
        if seg < 2:
            send_layer(seg + 1, a)

    for seg in range(3):

        def rate_step(j, carry):
            rate_layer(seg, j)
            return carry

        lax.fori_loop(0, LAYERS, rate_step, 0)

    for c in range(CHUNKS):
        each(lambda s: phase1(c, s).wait_send())
        each(lambda s: phase2(c, s).wait_send())
    for seg in range(3):
        for a in range(LAYERS):
            radial_copy(seg, a).wait_send()
        behind_copy(seg).wait_send()
        ahead_copy(seg).wait_send()


def per_device(coarse_state, send_cells, fine_source, weight, neighbours, face_area, time_step, mixing, frequency):
    vmem = pl.BlockSpec(memory_space=pltpu.VMEM)
    hbm = pl.BlockSpec(memory_space=pltpu.HBM)
    fine = pl.pallas_call(
        kernel,
        out_shape=jax.ShapeDtypeStruct((NI, NV, CELLS), F32),
        in_specs=[hbm] * 10,
        out_specs=vmem,
        scratch_shapes=[
            pltpu.VMEM((NI, NV, TILE), F32),
            pltpu.VMEM((1, CELLS), jnp.int32),
            pltpu.VMEM((2, CELLS), jnp.int32),
            pltpu.VMEM((1, CELLS), F32),
            pltpu.VMEM((6, CELLS), jnp.int32),
            pltpu.VMEM((6, CELLS), F32),
            pltpu.VMEM((1, CELLS), F32),
            pltpu.SMEM((NV, 6, NV), F32),
            pltpu.SMEM((1,), F32),
            pltpu.VMEM((SPLIT, SPLIT), BF16),
            pltpu.SemaphoreType.DMA((10,)),
            pltpu.VMEM((GROUP, ROWS, 128), F32),
            pltpu.VMEM((GROUP, ROWS, 128), F32),
            pltpu.VMEM((GROUP, ROWS, 128), F32),
            pltpu.VMEM((GROUP, ROWS, 128), F32),
            pltpu.VMEM((SPLIT // 16, SOURCES * 16, TILE), BF16),
            pltpu.VMEM((2, TILES, TILE, TILE), BF16),
            pltpu.VMEM((6, TILES, TILE, TILE), BF16),
            pltpu.VMEM((SPLIT // 16, 12 * 16, TILE), BF16),
            pltpu.VMEM((SPLIT // 16, 12 * 16, TILE), BF16),
            pltpu.VMEM((6, CELLS), jnp.int32),
            pltpu.VMEM((2, CELLS), jnp.int32),
            pltpu.VMEM((ROWS, CELLS + 3 * RIM), F32),
            pltpu.VMEM((ROWS, CELLS + 3 * RIM), F32),
            pltpu.VMEM((ROWS, CELLS + 3 * RIM), F32),
            pltpu.VMEM((6, NV, 8, 128), F32),
            pltpu.SemaphoreType.DMA((CHUNKS, GROUP)),
            pltpu.SemaphoreType.DMA((CHUNKS, GROUP)),
            pltpu.SemaphoreType.DMA((CHUNKS, GROUP)),
            pltpu.SemaphoreType.DMA((CHUNKS, GROUP)),
            pltpu.SemaphoreType.DMA((3, 6)),
            pltpu.SemaphoreType.DMA((3, 6)),
        ],
        compiler_params=pltpu.CompilerParams(
            collective_id=0, has_side_effects=True, vmem_limit_bytes=48 * 2**20
        ),
        name="grid_sequence",
    )(
        *[
            x if x.shape == (1,) else pltpu.with_memory_space_constraint(x, pltpu.HBM)
            for x in (
                coarse_state.transpose(1, 0, 2),
                send_cells,
                fine_source,
                weight.reshape(1, CELLS),
                neighbours,
                face_area,
                time_step.reshape(1, CELLS),
                mixing.transpose(1, 0, 2),
                frequency,
                jnp.asarray(spectral_rows()),
            )
        ]
    )
    return fine.transpose(1, 0, 2)


def solution(mesh):
    placed = (
        P(None, None, ("theta", "inst")),
        P(("theta", "inst"), None),
        P(None, ("theta", "inst")),
        P(("theta", "inst")),
        P(None, ("theta", "inst")),
        P(None, ("theta", "inst")),
        P(("theta", "inst")),
        P(),
        P(),
    )
    return jax.shard_map(
        per_device,
        mesh=mesh,
        in_specs=placed,
        out_specs=P(None, None, ("theta", "inst")),
        check_vma=False,
    )
```

```python
import functools

import jax
import jax.numpy as jnp
import numpy as np
from jax import lax
from jax.experimental import pallas as pl
from jax.experimental.pallas import tpu as pltpu
from jax.sharding import PartitionSpec as P

NV = 5
NI = 9
AXIAL = 128
RAD = 4
LAYERS = 4
RIM = 512
CELLS = 2048
EXT = CELLS + 2 * RIM
ROWS = 48
SPLIT = 2 * ROWS
TILE = 256
TILES = CELLS // TILE
NEAR = 7
NEAR_BLOCKS = 13
BY_MATRIX = 5
GROUP = 16
CHUNK = 24
CHUNKS = ROWS // CHUNK
FIRST = (8, 7, 9, 6, 10, 5, 11, 4, 12, 3, 13, 2, 14, 1, 15)
SOURCES = 8

SEGMENT_COEFS = (0.6, 0.6, 1.0)
MESH = pl.DeviceIdType.MESH
F32 = jnp.float32
BF16 = jnp.bfloat16


def spectral_rows():
    offsets = np.arange(NI)[:, None] - np.arange(NI)[None, :]
    sine = np.where(offsets == 0, 1.0, np.sin(np.pi * offsets / NI))
    matrix = np.where(offsets == 0, 0.0, 0.5 * np.where(offsets % 2 == 0, 1.0, -1.0) / sine)
    place = np.array([[v * 8 + n if n < 8 else NV * 8 + v for n in range(NI)] for v in range(NV)])
    full = np.zeros((ROWS, ROWS), np.float32)
    for v in range(NV):
        full[np.ix_(place[v], place[v])] = matrix
    high = full.astype(BF16)
    low = (full - high.astype(np.float32)).astype(BF16)
    twice = [np.concatenate([x[:, r : r + 16]] * 2, 1) for x in (high, low) for r in range(0, ROWS, 16)]
    return np.concatenate([np.concatenate(twice[:3], 1), np.concatenate(twice[3:], 1)], 0)


def halves(x):
    high = x.astype(BF16)
    return high, (x - high.astype(F32)).astype(BF16)


def one_hot(low):
    hit = lax.broadcasted_iota(jnp.int32, (TILE, TILE), 0) == low
    return jnp.where(hit, 1.0, 0.0).astype(BF16)


def pick(table, hot, sets, count):
    found = jnp.dot(table, hot, preferred_element_type=F32)
    sets = jnp.broadcast_to(sets, (8, TILE))
    masks = [sets == s for s in range(1, count)]
    rows = []
    for r in range(0, ROWS, 8):
        parts = []
        for half in range(2):
            base = ((r // 16) * 2 + half) * count * 16 + r % 16
            value = found[base : base + 8]
            for s in range(1, count):
                value = jnp.where(masks[s - 1], found[base + s * 16 : base + s * 16 + 8], value)
            parts.append(value)
        rows.append(parts[0] + parts[1])
    return rows


def from_block(block, place, masks, values):
    merged = []
    for r in range(ROWS // 8):
        rows = block(r)
        found = [
            jnp.take_along_axis(rows, jnp.broadcast_to(place[:, at : at + 128], (8, 128)), axis=1, mode="promise_in_bounds")
            for at in range(0, TILE, 128)
        ]
        merged.append(jnp.where(masks, jnp.concatenate(found, axis=1), values[r]))
    return merged


def kernel(
    coarse_in, send_in, fsrc_in, weight_in, nbr_in, area_in, dt_in, mix_in, freq_in, dmat_in, out,
    coarse, send, fsrc, weight, nbr, area, dt, mix, freq, dmat, isem, outg, recv1, send2, recv2, rtab, ohs, ohn, near0, near1, sidn, sids, field0, field1, field2, mixcol,
    ssem1, rsem1, ssem2, rsem2, hssem, hrsem,
):
    inputs = [
        pltpu.make_async_copy(src, dst, isem.at[at])
        for at, (src, dst) in enumerate(
            [
                (coarse_in, coarse), (send_in, send), (fsrc_in, fsrc), (nbr_in, nbr), (mix_in, mix),
                (freq_in, freq), (weight_in, weight), (area_in, area), (dt_in, dt), (dmat_in, dmat),
            ]
        )
    ]
    for copy in inputs:
        copy.start()

    field = [field0, field1, field2]
    near = [near0, near1]
    t = lax.axis_index("theta")
    i = lax.axis_index("inst")
    count = 128
    z, x_lo, y, core = t // 16, t // 8 % 2, t // 2 % 4, t % 2
    g = z * 2 + core
    h = y * 4 + x_lo * 2 + i

    def in_phase1(s):
        other = (g + s) % GROUP
        return ((other // 2 * 2 + x_lo) * 4 + y) * 2 + other % 2, i

    def in_phase2(s):
        other = (h + s) % GROUP
        return ((z * 2 + other // 2 % 2) * 4 + other // 4) * 2 + core, other % 2

    ahead = ((t + 1) % count, i)
    behind = ((t + count - 1) % count, i)
    partner = (t, 1 - i)

    def lanes(start, size):
        return pl.ds(pl.multiple_of(start, 128), size)

    for arriving in (recv1, recv2):
        arriving[:, ROWS - 8 :, :] = jnp.zeros((GROUP, 8, 128), F32)
    barrier = pltpu.get_barrier_semaphore()

    def greet(s, carry):
        pl.semaphore_signal(barrier, inc=1, device_id=in_phase1(s), device_id_type=MESH)
        pl.semaphore_signal(barrier, inc=1, device_id=in_phase2(s), device_id_type=MESH)
        return carry

    lax.fori_loop(1, GROUP, greet, 0)
    pl.semaphore_signal(barrier, inc=1, device_id=ahead, device_id_type=MESH)
    pl.semaphore_signal(barrier, inc=1, device_id=behind, device_id_type=MESH)

    inputs[0].wait()
    inputs[1].wait()

    rows = jnp.concatenate(
        [coarse[0:8, v, :] for v in range(NV)] + [coarse[8], jnp.zeros((ROWS - NV * NI, TILE), F32)], axis=0
    )
    table = jnp.concatenate(halves(rows), axis=0)

    lane = lax.broadcasted_iota(jnp.int32, (8, 128), 1)

    for c in range(TILES):
        even = send[:, lanes(c * TILE, 128)]
        odd = send[:, lanes(c * TILE + 128, 128)]
        keep = (lane[:1] & 16) == 0
        first = jnp.where(keep, even, pltpu.roll(odd, 16, 1))
        second = jnp.where(keep, pltpu.roll(even, 112, 1), odd)
        low = jnp.maximum(jnp.concatenate([first, second], axis=1), 0)
        found = jnp.dot(table, one_hot(low), preferred_element_type=F32)
        found = found[:ROWS] + found[ROWS:]
        outg[2 * c] = found[:, :128]
        outg[2 * c + 1] = found[:, 128:]

    pl.semaphore_wait(barrier, 2 * (GROUP - 1) + 2)

    def phase1(c, s):
        part = pl.ds(c * CHUNK, min(CHUNK, NV * NI - c * CHUNK))
        return pltpu.make_async_remote_copy(
            src_ref=outg.at[(g + s) % GROUP, part],
            dst_ref=recv1.at[g, part],
            send_sem=ssem1.at[c, s],
            recv_sem=rsem1.at[c, s],
            device_id=in_phase1(s),
            device_id_type=MESH,
        )

    def phase2(c, s):
        part = pl.ds(c * CHUNK, min(CHUNK, NV * NI - c * CHUNK))
        return pltpu.make_async_remote_copy(
            src_ref=send2.at[(h + s) % GROUP, part],
            dst_ref=recv2.at[h, part],
            send_sem=ssem2.at[c, s],
            recv_sem=rsem2.at[c, s],
            device_id=in_phase2(s),
            device_id_type=MESH,
        )

    def each(action):
        for s in range(1, GROUP):
            action(s)

    for c in range(CHUNKS):
        for s in FIRST:
            phase1(c, s).start()
    recv1[g] = outg[g]

    for copy in inputs[2:5]:
        copy.wait()

    slots = fsrc[...]
    owner = slots >> 3
    from_g = (owner >> 5) * 2 + ((owner >> 1) & 1)
    from_h = ((owner >> 2) & 3) * 4 + ((owner >> 4) & 1) * 2 + (owner & 1)
    places = from_h * 128 + from_g * 8 + (slots & 7)
    low_places = places & 255
    sids[...] = places >> 8
    fsrc[...] = low_places
    links = nbr[...]
    layer = lax.broadcasted_iota(jnp.int32, (6, CELLS), 1) >> 9
    sidn[...] = jnp.where(links >= EXT, NEAR - 1, (links >> 8) - 2 * layer)

    def hot_start(c, carry):
        cells = pl.ds(pl.multiple_of(c * TILE, TILE), TILE)
        for side in range(2):
            ohs[side, c] = one_hot(fsrc[side : side + 1, cells])
        for k in range(6):
            ohn[k, c] = one_hot(nbr[k : k + 1, cells] & 255)
        return carry

    lax.fori_loop(0, TILES, hot_start, 0)
    sub = lax.broadcasted_iota(jnp.int32, (8, 128), 0)
    for k in range(6):
        for w in range(NV):
            column = jnp.zeros((8, 128), F32)
            for v in range(NV):
                column = jnp.where(sub == v, mix[v, k, w], column)
            mixcol[k, w] = column

    for c in range(CHUNKS):
        each(lambda s: phase1(c, s).wait_recv())
        for r in range(CHUNK // 8):
            part = pl.ds(c * CHUNK + 8 * r, 8)
            x = [recv1[j, part, :] for j in range(GROUP)]
            for bit in range(4):
                step = 8 << bit
                keep = (lane & step) == 0
                for a in range(GROUP):
                    b = a | (1 << bit)
                    if a != b:
                        low = jnp.where(keep, x[a], pltpu.roll(x[b], step, 1))
                        high = jnp.where(keep, pltpu.roll(x[a], 128 - step, 1), x[b])
                        x[a], x[b] = low, high
            for j in range(GROUP):
                send2[j, part, :] = x[j]
        for s in FIRST:
            phase2(c, s).start()
    recv2[h] = send2[h]
    for c in range(CHUNKS):
        each(lambda s: phase2(c, s).wait_recv())

    for s in range(SOURCES):
        for side in range(2):
            for half, values in enumerate(halves(recv2[2 * s + side])):
                for r in range(ROWS // 16):
                    rtab[2 * r + half, 16 * s : 16 * s + 16, side * 128 : side * 128 + 128] = values[16 * r : 16 * r + 16]

    my_row = jnp.where(i == 0, RAD - 1, 0) * AXIAL

    def radial_copy(seg, a):
        return pltpu.make_async_remote_copy(
            src_ref=field[seg].at[:, lanes(RIM + a * RIM + my_row, AXIAL)],
            dst_ref=field[seg].at[:, lanes(EXT + a * AXIAL, AXIAL)],
            send_sem=hssem.at[seg, a],
            recv_sem=hrsem.at[seg, a],
            device_id=partner,
            device_id_type=MESH,
        )

    def behind_copy(seg):
        return pltpu.make_async_remote_copy(
            src_ref=field[seg].at[:, pl.ds(RIM, RIM)],
            dst_ref=field[seg].at[:, pl.ds(RIM + CELLS, RIM)],
            send_sem=hssem.at[seg, 4],
            recv_sem=hrsem.at[seg, 4],
            device_id=behind,
            device_id_type=MESH,
        )

    def ahead_copy(seg):
        return pltpu.make_async_remote_copy(
            src_ref=field[seg].at[:, pl.ds(CELLS, RIM)],
            dst_ref=field[seg].at[:, pl.ds(0, RIM)],
            send_sem=hssem.at[seg, 5],
            recv_sem=hrsem.at[seg, 5],
            device_id=ahead,
            device_id_type=MESH,
        )

    def send_layer(seg, a):
        radial_copy(seg, a).start()

        @pl.when(a == 0)
        def _():
            behind_copy(seg).start()

        @pl.when(a == LAYERS - 1)
        def _():
            ahead_copy(seg).start()

    def put(side, at, values):
        for half, part in enumerate(halves(jnp.concatenate(values, axis=0))):
            for r in range(ROWS // 16):
                near[side][2 * r + half, pl.ds(pl.multiple_of(at * 16, 16), 16), :] = part[16 * r : 16 * r + 16]

    def layer_of(seg, j):
        outer = (j - 2) * 3 if seg % 2 == 0 else (3 - j) * 3
        return jnp.where(j < 2, j + 1, outer)

    for copy in inputs[5:]:
        copy.wait()

    def start_layer(j, carry):
        a = layer_of(1, j)
        for half in range(2):
            c = 2 * a + half
            cells = lanes(c * TILE, TILE)
            first = pick(rtab[...].reshape(SOURCES * SPLIT, TILE), ohs[0, c], sids[0:1, cells], SOURCES)
            second = pick(rtab[...].reshape(SOURCES * SPLIT, TILE), ohs[1, c], sids[1:2, cells], SOURCES)
            share = jnp.broadcast_to(weight[:, cells], (8, TILE))
            begin = [share * x + (1.0 - share) * y for x, y in zip(first, second)]
            for r in range(ROWS // 8):
                field[0][8 * r : 8 * r + 8, lanes(RIM + c * TILE, TILE)] = begin[r]
            put(0, 2 + c, begin)
        send_layer(0, a)
        return carry

    lax.fori_loop(0, LAYERS, start_layer, 0)

    omega = freq[0]

    def rate_tile(seg, side, coef, a, half):
        c = 2 * a + half
        cells = lanes(c * TILE, TILE)
        here = lanes(RIM + c * TILE, TILE)
        own = [field[seg][8 * r : 8 * r + 8, here] for r in range(ROWS // 8)]
        mine = near[side][:, pl.ds(pl.multiple_of((2 + c) * 16, 16), 16), :].reshape(SPLIT, TILE)
        turned = jnp.dot(dmat[...], mine, preferred_element_type=F32)
        rate = [omega * (turned[8 * r : 8 * r + 8] + turned[ROWS + 8 * r : ROWS + 8 * r + 8]) for r in range(ROWS // 8)]
        table = near[side][:, pl.ds(pl.multiple_of(2 * a * 16, 16), BY_MATRIX * 16), :].reshape(BY_MATRIX * SPLIT, TILE)

        def block(start):
            return lambda r: field[seg][8 * r : 8 * r + 8, lanes(start, 128)]

        for k in range(6):
            links = nbr[k : k + 1, cells]
            sets = jnp.broadcast_to(sidn[k : k + 1, cells], (8, TILE))
            found = pick(table, ohn[k, c], sets, BY_MATRIX)
            place = links & 127
            for s in range(2 * BY_MATRIX, NEAR_BLOCKS - 1):
                start = a * RIM + s * 128
                found = from_block(block(start), place, jnp.broadcast_to(links >> 7, (8, TILE)) == 4 * a + s, found)
            found = from_block(block(EXT + a * AXIAL), place, sets == NEAR - 1, found)
            face = jnp.broadcast_to(area[k : k + 1, cells], (8, TILE))
            jump = [(found[r] - own[r]) * face for r in range(ROWS // 8)]
            for v in range(NV):
                flux = mix[v, k, 0] * jump[0]
                for w in range(1, NV):
                    flux = flux + mix[v, k, w] * jump[w]
                rate[v] = rate[v] - flux
            last = jnp.zeros((8, TILE), F32)
            for w in range(NV):
                column = mixcol[k, w]
                last = last + jnp.concatenate([column, column], axis=1) * jnp.broadcast_to(jump[NV][w : w + 1], (8, TILE))
            rate[NV] = rate[NV] - last
        step = jnp.broadcast_to(coef * dt[:, cells], (8, TILE))
        after = [field[0][8 * r : 8 * r + 8, here] - step * rate[r] for r in range(ROWS // 8)]
        if seg < 2:
            for r in range(ROWS // 8):
                field[seg + 1][8 * r : 8 * r + 8, here] = after[r]
            put(1 - side, 2 + c, after)
        else:
            for v in range(NV):
                out[0:8, v, cells] = after[v]
            out[8, :, cells] = after[NV][:NV]

    def rate_layer(seg, j):
        side = seg % 2
        a = layer_of(seg, j)

        def arrived(start, at_set):
            for half in range(2):
                put(side, at_set + half, [field[seg][:, start + half * TILE : start + (half + 1) * TILE]])

        @pl.when(a == 0)
        def _():
            ahead_copy(seg).wait_recv()
            arrived(0, 0)

        @pl.when(a == LAYERS - 1)
        def _():
            behind_copy(seg).wait_recv()
            arrived(RIM + CELLS, 10)

        radial_copy(seg, a).wait_recv()
        for half in range(2):
            rate_tile(seg, side, SEGMENT_COEFS[seg], a, half)
        if seg < 2:
            send_layer(seg + 1, a)

    for seg in range(3):

        def rate_step(j, carry):
            rate_layer(seg, j)
            return carry

        lax.fori_loop(0, LAYERS, rate_step, 0)

    for c in range(CHUNKS):
        each(lambda s: phase1(c, s).wait_send())
        each(lambda s: phase2(c, s).wait_send())
    for seg in range(3):
        for a in range(LAYERS):
            radial_copy(seg, a).wait_send()
        behind_copy(seg).wait_send()
        ahead_copy(seg).wait_send()


def per_device(coarse_state, send_cells, fine_source, weight, neighbours, face_area, time_step, mixing, frequency):
    vmem = pl.BlockSpec(memory_space=pltpu.VMEM)
    hbm = pl.BlockSpec(memory_space=pltpu.HBM)
    fine = pl.pallas_call(
        kernel,
        out_shape=jax.ShapeDtypeStruct((NI, NV, CELLS), F32),
        in_specs=[hbm] * 10,
        out_specs=vmem,
        scratch_shapes=[
            pltpu.VMEM((NI, NV, TILE), F32),
            pltpu.VMEM((1, CELLS), jnp.int32),
            pltpu.VMEM((2, CELLS), jnp.int32),
            pltpu.VMEM((1, CELLS), F32),
            pltpu.VMEM((6, CELLS), jnp.int32),
            pltpu.VMEM((6, CELLS), F32),
            pltpu.VMEM((1, CELLS), F32),
            pltpu.SMEM((NV, 6, NV), F32),
            pltpu.SMEM((1,), F32),
            pltpu.VMEM((SPLIT, SPLIT), BF16),
            pltpu.SemaphoreType.DMA((10,)),
            pltpu.VMEM((GROUP, ROWS, 128), F32),
            pltpu.VMEM((GROUP, ROWS, 128), F32),
            pltpu.VMEM((GROUP, ROWS, 128), F32),
            pltpu.VMEM((GROUP, ROWS, 128), F32),
            pltpu.VMEM((SPLIT // 16, SOURCES * 16, TILE), BF16),
            pltpu.VMEM((2, TILES, TILE, TILE), BF16),
            pltpu.VMEM((6, TILES, TILE, TILE), BF16),
            pltpu.VMEM((SPLIT // 16, 12 * 16, TILE), BF16),
            pltpu.VMEM((SPLIT // 16, 12 * 16, TILE), BF16),
            pltpu.VMEM((6, CELLS), jnp.int32),
            pltpu.VMEM((2, CELLS), jnp.int32),
            pltpu.VMEM((ROWS, CELLS + 3 * RIM), F32),
            pltpu.VMEM((ROWS, CELLS + 3 * RIM), F32),
            pltpu.VMEM((ROWS, CELLS + 3 * RIM), F32),
            pltpu.VMEM((6, NV, 8, 128), F32),
            pltpu.SemaphoreType.DMA((CHUNKS, GROUP)),
            pltpu.SemaphoreType.DMA((CHUNKS, GROUP)),
            pltpu.SemaphoreType.DMA((CHUNKS, GROUP)),
            pltpu.SemaphoreType.DMA((CHUNKS, GROUP)),
            pltpu.SemaphoreType.DMA((3, 6)),
            pltpu.SemaphoreType.DMA((3, 6)),
        ],
        compiler_params=pltpu.CompilerParams(
            collective_id=0, has_side_effects=True, vmem_limit_bytes=48 * 2**20
        ),
        name="grid_sequence",
    )(
        *[
            x if x.shape == (1,) else pltpu.with_memory_space_constraint(x, pltpu.HBM)
            for x in (
                coarse_state.transpose(1, 0, 2),
                send_cells,
                fine_source,
                weight.reshape(1, CELLS),
                neighbours,
                face_area,
                time_step.reshape(1, CELLS),
                mixing.transpose(1, 0, 2),
                frequency,
                jnp.asarray(spectral_rows()),
            )
        ]
    )
    return fine.transpose(1, 0, 2)


def solution(mesh):
    placed = (
        P(None, None, ("theta", "inst")),
        P(("theta", "inst"), None),
        P(None, ("theta", "inst")),
        P(("theta", "inst")),
        P(None, ("theta", "inst")),
        P(None, ("theta", "inst")),
        P(("theta", "inst")),
        P(),
        P(),
    )
    return jax.shard_map(
        per_device,
        mesh=mesh,
        in_specs=placed,
        out_specs=P(None, None, ("theta", "inst")),
        check_vma=False,
    )
```
